128 devices in a mesh: frame: 16 (over x, y), expert: 8 (over z, core).
Axes of the slice: x: 4, y: 4, z: 4, core: 2. Of those that a mesh axis runs over, the one named last changes fastest.
Arguments:
- patches: bfloat16 [16, 8, 256, 1536], P('frame', 'expert'), may hold values from -6 to 6
- temporal_q: bfloat16 [16, 8, 256, 1536], P('frame', 'expert'), may hold values from -70 to 70
- temporal_k: bfloat16 [16, 8, 256, 1536], P('frame', 'expert'), may hold values from -6 to 6
- temporal_v: bfloat16 [16, 8, 256, 1536], P('frame', 'expert'), may hold values from -6 to 6
- clip_lengths: int32 [8], P('expert'), may hold values from 1 to 16
- w_time: bfloat16 [1536, 1536], replicated, may hold values from -0.15625 to 0.15625
- gain_space: float32 [1536], replicated, may hold values from 0.1 to 1.9
- w_space: bfloat16 [1536, 4608], P(None, 'frame'), may hold values from -2 to 2
- w_merge: bfloat16 [1536, 1536], replicated, may hold values from -0.15625 to 0.15625
- gain_mix: float32 [1536], replicated, may hold values from 0.1 to 1.9
- expert_ids: int32 [16, 8, 256, 2], P('frame', 'expert'), may hold values from 0 to 31, all different within a row; in each aligned block of 256 rows (0 to 255, 256 to 511, ..., all dimensions but the last counted through in order) at most 18 rows name the same one
- gate_weights: float32 [16, 8, 256, 2], P('frame', 'expert'), may hold values from 0.25 to 1
- w_expand: bfloat16 [128, 1536, 1536], P(('frame', 'expert')), may hold values from -0.15625 to 0.15625
- w_reduce: bfloat16 [128, 1536, 1536], P(('frame', 'expert')), may hold values from -0.078125 to 0.078125
Outputs:
- block_out: bfloat16 [16, 8, 256, 1536], P('frame', 'expert')
The draws below stay inside these ranges and needn't reach their ends.
Inputs may be any that keep to these rules, and one draw needn't show every extreme that they name: `expert_ids`: the rows of one device (the 256 rows of one frame and 1 clips) name no expert more than 18 times, and in some device's rows an expert is named exactly 18 times; the two experts of a row differ.
All inputs are finite; a program needn't handle non-finite values.
Results may differ from the reference program's by a relative error of at most 0.0065.
Values may be sent and summed in bfloat16 or wider, within the bound.
No kernel may reach another device: no remote copies, remote signals or barrier semaphores. Data moves between devices by JAX's collectives and lax.ppermute only.
A program may use at most 128 MiB of HBM per device.

```python
import math
import jax
import jax.numpy as jnp
import numpy as np
from jax import lax

D = 1536
HEADS = 24
FF_EXPERT = 6144
EXPERTS = 32
PATCHES = 256
FRAMES = 16
CLIPS = 8
ROWS_DEV = 256
CAP = 18
SHARDS = 4
HID_DEV = 1536
DEVICES = 128


def query_key_pair(key):
    full_shape = (FRAMES, CLIPS, PATCHES, D)
    key_rows = jnp.clip(jax.random.normal(jax.random.fold_in(key, 11), full_shape, jnp.float32), -6.0, 6.0)
    queries = jnp.clip(jax.random.normal(jax.random.fold_in(key, 12), full_shape, jnp.float32), -6.0, 6.0)
    return (queries, key_rows)


def draw_temporal_q(key, part):
    return query_key_pair(key)[0].astype(jnp.bfloat16)


def draw_temporal_k(key, part):
    return query_key_pair(key)[1].astype(jnp.bfloat16)


def draw_w_space(key, part):
    factor = D ** (-0.5)
    base = jax.random.normal(jax.random.fold_in(key, 21), (D, 3 * D), jnp.float32) * factor
    return base.astype(jnp.bfloat16)


def plant(array, stream_key, low, largest):
    index_at = [jax.random.randint(jax.random.fold_in(stream_key, axis), (), 0, length) for axis, length in enumerate(array.shape)]
    main_axis = array.shape.index(max(array.shape))
    beside = index_at[:main_axis] + [(index_at[main_axis] + 1) % array.shape[main_axis]] + index_at[main_axis + 1:]
    return array.at[tuple(index_at)].set(low).at[tuple(beside)].set(largest)


def block_scale(stream_key, extent, shards, smallest, largest):
    factor_of, own = 1.0, jax.random.fold_in(stream_key, 6)
    for axis_at, shards_of in shards:
        draws = jnp.exp(jax.random.uniform(jax.random.fold_in(own, axis_at), (shards_of,), jnp.float32, smallest / len(shards), largest / len(shards)))
        factor_of = factor_of * jnp.repeat(draws, extent[axis_at] // shards_of).reshape([-1 if axis == axis_at else 1 for axis in range(len(extent))])
    return factor_of


def routed_block(own_key, own, number, rows, amount, top, most, skew):
    ranking = jax.random.permutation(own_key, amount)
    crowded, usual = portions_of(amount, rows * top, most, skew, True), portions_of(amount, rows * top, most, skew, False)
    places = jnp.arange(amount)

    def named(lengths, rotation):
        used = int((lengths > 0).sum())
        fixed = max(1, used // 4)
        shifted = fixed + (places - fixed + rotation * (used - fixed)) % max(1, amount - fixed)
        return jnp.zeros((amount,), jnp.int32).at[ranking[jnp.where(places < fixed, places, shifted)]].set(jnp.asarray(lengths, jnp.int32))

    lengths = jnp.where(number % 4 == 0, named(crowded, number // 4), named(usual, number - number // 4 - 1))
    mixed = jax.random.permutation(jax.random.fold_in(own, 3), amount)
    giver, sink = mixed[0:amount // 2 * 2:2], mixed[1:amount // 2 * 2:2]
    room = jnp.minimum(lengths[giver] - 1, most - lengths[sink]) // 2
    room = jnp.where((giver == ranking[0]) | (sink == ranking[0]) | (lengths[sink] == 0), 0, jnp.maximum(room, 0))
    shifted = jax.random.randint(jax.random.fold_in(own, 4), (amount // 2,), 0, 1 << 20) % (room + 1)
    lengths = lengths.at[giver].add(-shifted).at[sink].add(shifted)
    labels = jnp.searchsorted(jnp.cumsum(lengths), jnp.arange(rows * top), side="right").astype(jnp.int32)
    grid = labels.reshape(top, rows).T
    grid = grid[jax.random.permutation(jax.random.fold_in(own, 1), rows)]
    rotation = jax.random.randint(jax.random.fold_in(own, 2), (rows, 1), 0, top)
    return jnp.take_along_axis(grid, (jnp.arange(top)[None, :] + rotation) % top, axis=1)


def portions_of(number_of, total, reach, skew, full):
    portions = [(1 << 20) // math.isqrt(standing ** skew) + 1 for standing in range(1, number_of + 1)]
    largest = reach if full else min(reach, max(-(-total // number_of), total * portions[0] // sum(portions)))
    least = 1 if total - largest >= number_of - 1 else 0
    given, surplus = [largest] + [least] * (number_of - 1), total - largest - least * (number_of - 1)
    while surplus > 0:
        movable = [i for i in range(1, number_of) if given[i] < largest] or [i for i in range(1, number_of) if given[i] < reach]
        mass, budget = sum([portions[i] for i in movable]), surplus
        for i in movable:
            addition = min(reach - given[i], max(1, budget * portions[i] // mass), surplus)
            given[i] = given[i] + addition
            surplus = surplus - addition
    return np.array(given)


def scatter_about(rng, dims, deviation, limit, pieces=(), kind=jnp.bfloat16):
    factor_of = block_scale(rng, dims, pieces, -0.22, 0.18) if pieces else 1.0
    array = jax.random.normal(rng, dims, jnp.float32) * deviation * factor_of
    return jnp.minimum(jnp.maximum(array, -limit), limit).astype(kind)


def setup_inputs(seed: int = 0) -> dict:
    keys = jax.random.split(jax.random.key(seed), 15)
    patches = scatter_about(keys[0], (FRAMES, CLIPS, PATCHES, D), 1.0, 6.0, ((0, 16), (1, 8)))
    temporal_q = draw_temporal_q(jax.random.fold_in(keys[14], 71), 0)
    temporal_k = draw_temporal_k(jax.random.fold_in(keys[14], 71), 0)
    temporal_v = scatter_about(keys[3], (FRAMES, CLIPS, PATCHES, D), 1.0, 6.0, ((0, 16), (1, 8)))
    clip_lengths = plant(jax.random.randint(keys[4], (CLIPS,), 1, FRAMES + 1), jax.random.fold_in(keys[4], 1), 1, FRAMES).astype(jnp.int32)
    w_time = scatter_about(keys[5], (D, D), D ** -0.5, 0.15625)
    gain_space = jnp.clip(1.0 + 0.18 * jax.random.normal(keys[6], (D,), jnp.float32), 0.1, 1.9)
    w_space = draw_w_space(jax.random.fold_in(keys[14], 71), 0)
    w_merge = scatter_about(keys[8], (D, D), D ** -0.5, 0.15625)
    gain_mix = jnp.clip(1.0 + 0.18 * jax.random.normal(keys[9], (D,), jnp.float32), 0.1, 1.9)
    expert_ids_keys = jax.random.split(jax.random.fold_in(keys[10], 1), FRAMES * CLIPS * PATCHES // ROWS_DEV)
    expert_ids_turns = jax.random.permutation(jax.random.fold_in(keys[10], 3), FRAMES * CLIPS * PATCHES // ROWS_DEV)
    expert_ids = jax.vmap(lambda own, number: routed_block(jax.random.fold_in(keys[10], 2), own, number, ROWS_DEV, EXPERTS, 2, CAP, 2))(expert_ids_keys, expert_ids_turns).reshape((FRAMES, CLIPS, PATCHES, 2))
    gate_weights = jnp.clip(0.25 + 0.75 * jax.random.uniform(keys[11], (FRAMES, CLIPS, PATCHES, 2), jnp.float32) ** block_scale(keys[11], (FRAMES, CLIPS, PATCHES, 2), ((0, 16), (1, 8)), -0.2, 0.2), 0.25, 1.0)
    w_expand = scatter_about(keys[12], (DEVICES, D, HID_DEV), D ** -0.5, 0.15625, ((0, 128),))
    w_reduce = scatter_about(keys[13], (DEVICES, HID_DEV, D), FF_EXPERT ** -0.5, 0.078125, ((0, 128),))
    return dict(patches=patches, temporal_q=temporal_q, temporal_k=temporal_k, temporal_v=temporal_v, clip_lengths=clip_lengths, w_time=w_time, gain_space=gain_space, w_space=w_space, w_merge=w_merge, gain_mix=gain_mix, expert_ids=expert_ids, gate_weights=gate_weights, w_expand=w_expand, w_reduce=w_reduce)


epsilon = 1e-06

def layer_norm(values, gain_vector):
    centre = values - lax.optimization_barrier(jnp.mean(values, axis=-1, keepdims=True))
    spread = lax.optimization_barrier(jnp.mean(centre * centre, axis=-1, keepdims=True))
    return (centre * lax.rsqrt(spread + epsilon) * gain_vector.astype(jnp.float32)).astype(jnp.bfloat16)

def softmax_rows(scores):
    top_score = lax.optimization_barrier(jnp.max(scores, axis=-1, keepdims=True))
    powers = jnp.exp(scores - top_score)
    return (powers / lax.optimization_barrier(jnp.sum(powers, axis=-1, keepdims=True))).astype(jnp.bfloat16)

def time_attention(queries, key_rows, value_rows, clip_lengths):
    frame_count, clip_count, place_count, model_width = queries.shape
    head_size = model_width // HEADS

    def split_heads(array_in):
        return array_in.astype(jnp.float32).reshape(frame_count, clip_count, place_count, HEADS, head_size)
    scores = jnp.einsum('fcphd,gcphd->cphfg', split_heads(queries), split_heads(key_rows)) / math.sqrt(head_size)
    valid_keys = jnp.arange(frame_count, dtype=jnp.int32)[None, :] < clip_lengths[:, None]
    scores = jnp.where(valid_keys[:, None, None, None, :], scores, -1e+30)
    weights = softmax_rows(scores)
    attended = jnp.einsum('cphfg,gcphd->fcphd', weights.astype(jnp.float32), split_heads(value_rows))
    return attended.astype(jnp.bfloat16).reshape(frame_count, clip_count, place_count, model_width)

def space_attention(projected):
    clip_count, place_count, triple = projected.shape
    model_width = triple // 3
    head_size = model_width // HEADS
    split_parts = projected.astype(jnp.float32).reshape(clip_count, place_count, 3, HEADS, head_size)
    scores = jnp.einsum('cphd,cqhd->chpq', split_parts[:, :, 0], split_parts[:, :, 1]) / math.sqrt(head_size)
    weights = softmax_rows(scores)
    attended = jnp.einsum('chpq,cqhd->cphd', weights.astype(jnp.float32), split_parts[:, :, 2])
    return attended.astype(jnp.bfloat16).reshape(clip_count, place_count, model_width)

def expert_slots(routes):
    onehot = (routes[..., None] == jnp.arange(EXPERTS, dtype=jnp.int32)).astype(jnp.int32)
    earlier = jnp.cumsum(onehot, axis=-2) - onehot
    return lax.optimization_barrier(jnp.sum(earlier * onehot, axis=-1)).astype(jnp.int32)

def reference(patches, temporal_q, temporal_k, temporal_v, clip_lengths, w_time, gain_space, w_space, w_merge, gain_mix, expert_ids, gate_weights, w_expand, w_reduce):
    model_width = D
    full_shape = patches.shape
    time_mixed = time_attention(temporal_q, temporal_k, temporal_v, clip_lengths)
    after_time = patches.astype(jnp.float32) + jnp.dot(time_mixed.reshape(-1, model_width), w_time, preferred_element_type=jnp.float32).reshape(full_shape)
    normed = layer_norm(after_time, gain_space).reshape(-1, model_width)
    projected = jnp.dot(normed, w_space, preferred_element_type=jnp.float32).astype(jnp.bfloat16)
    projected = projected.reshape(FRAMES, CLIPS, PATCHES, 3 * model_width)
    spatial = lax.map(space_attention, projected)
    after_space = after_time + jnp.dot(spatial.reshape(-1, model_width), w_merge, preferred_element_type=jnp.float32).reshape(full_shape)
    mixed_in = layer_norm(after_space, gain_mix).reshape(DEVICES, ROWS_DEV, model_width)
    routes = expert_ids.reshape(DEVICES, ROWS_DEV * 2).astype(jnp.int32)
    slot_index = expert_slots(routes)
    owner_index = jnp.arange(DEVICES, dtype=jnp.int32)[:, None]
    position = ((routes * DEVICES + owner_index) * CAP + slot_index).reshape(-1).astype(jnp.int32)
    sources = jnp.repeat(mixed_in, 2, axis=1).reshape(-1, model_width)
    buffer_rows = jnp.zeros((EXPERTS * DEVICES * CAP, model_width), jnp.bfloat16).at[position].set(sources)
    expand = w_expand.reshape(EXPERTS, SHARDS, model_width, HID_DEV)
    reduce_part = w_reduce.reshape(EXPERTS, SHARDS, HID_DEV, model_width)

    def run_expert(operands):
        token_rows, expand_blocks, reduce_blocks = operands
        running_sum = jnp.zeros((token_rows.shape[0], model_width), jnp.float32)
        for shard_index in range(SHARDS):
            hidden = jax.nn.gelu(jnp.dot(token_rows, expand_blocks[shard_index], preferred_element_type=jnp.float32), approximate=False).astype(jnp.bfloat16)
            partial_rows = jnp.dot(hidden, reduce_blocks[shard_index], preferred_element_type=jnp.float32).astype(jnp.bfloat16)
            running_sum = running_sum + lax.optimization_barrier(partial_rows).astype(jnp.float32)
        return running_sum
    results = lax.map(run_expert, (buffer_rows.reshape(EXPERTS, DEVICES * CAP, model_width), expand, reduce_part))
    picked = results.reshape(-1, model_width)[position].reshape(DEVICES, ROWS_DEV, 2, model_width)
    gate_rows = gate_weights.reshape(DEVICES, ROWS_DEV, 2, 1)
    expert_mix = picked[:, :, 0] * gate_rows[:, :, 0] + picked[:, :, 1] * gate_rows[:, :, 1]
    return (after_space + expert_mix.reshape(full_shape)).astype(jnp.bfloat16)
```

```python
import math

import jax
import jax.numpy as jnp
from jax import lax
from jax.experimental import pallas as pl
from jax.experimental.pallas import tpu as pltpu
from jax.sharding import Mesh, PartitionSpec as P

HEADS = 24
HEAD = 64
EXPERTS = 32
D = 1536
ROWS = 256
FRAMES = 16
MAIN = 16
PACK = 224
BLOCKS = D // 128
EPSILON = 1e-06
F32 = jnp.float32
BF16 = jnp.bfloat16
MIB = 1 << 20


def dot(a, b):
    return jnp.dot(a, b, preferred_element_type=F32)


def dot_nt(a, b):
    return lax.dot_general(a, b, (((1,), (1,)), ((), ())), preferred_element_type=F32)


def norm_rows(values, gain):
    centre = values - jnp.mean(values, axis=-1, keepdims=True)
    spread = jnp.mean(centre * centre, axis=-1, keepdims=True)
    return (centre * lax.rsqrt(spread + EPSILON) * gain).astype(BF16)


def time_kernel(len_ref, x_ref, o_ref):
    q = x_ref[:, 0:16, :].reshape(ROWS, 128)
    k = x_ref[:, 16:32, :].reshape(ROWS, 128)
    v = x_ref[:, 32:48, :].reshape(ROWS, 128)
    row = lax.broadcasted_iota(jnp.int32, (ROWS, ROWS), 0)
    col = lax.broadcasted_iota(jnp.int32, (ROWS, ROWS), 1)
    keep = ((row & 15) == (col & 15)) & ((col >> 4) < len_ref[0])
    low = lax.broadcasted_iota(jnp.int32, (ROWS, 128), 1) < HEAD
    zero = jnp.zeros((ROWS, 128), BF16)
    total = None
    for head in range(2):
        mine = low if head == 0 else ~low
        scores = dot_nt(q, jnp.where(mine, k, zero)) * (1.0 / math.sqrt(HEAD))
        scores = jnp.where(keep, scores, -1e30)
        powers = jnp.exp(scores - jnp.max(scores, axis=-1, keepdims=True))
        weights = (powers * (1.0 / jnp.sum(powers, axis=-1, keepdims=True))).astype(BF16)
        part = dot(weights, jnp.where(mine, v, zero))
        total = part if total is None else total + part
    o_ref[...] = total.astype(BF16).reshape(FRAMES, 16, 128)


def time_attention(lengths, qkv):
    return pl.pallas_call(
        time_kernel,
        grid=(BLOCKS,),
        in_specs=[
            pl.BlockSpec(memory_space=pltpu.SMEM),
            pl.BlockSpec((FRAMES, 48, 128), lambda i: (0, 0, i)),
        ],
        out_specs=pl.BlockSpec((FRAMES, 16, 128), lambda i: (0, 0, i)),
        out_shape=jax.ShapeDtypeStruct((FRAMES, 16, D), BF16),
        name="time_attention",
    )(lengths, qkv)


def after_time_kernel(mixed_ref, patch_ref, w_ref, gain_ref, after_ref, normed_ref):
    step = pl.program_id(0)
    cols = pl.ds(pl.multiple_of(step * 512, 512), 512)
    after_ref[:, cols] = patch_ref[...].astype(F32) + dot(mixed_ref[...], w_ref[...])

    @pl.when(step == 2)
    def _():
        normed_ref[...] = norm_rows(after_ref[...], gain_ref[...])


def after_time_step(mixed, patches, w_time, gain):
    return pl.pallas_call(
        after_time_kernel,
        grid=(3,),
        in_specs=[
            pl.BlockSpec((ROWS, D), lambda i: (0, 0)),
            pl.BlockSpec((ROWS, 512), lambda i: (0, i)),
            pl.BlockSpec((D, 512), lambda i: (0, i)),
            pl.BlockSpec((1, D), lambda i: (0, 0)),
        ],
        out_specs=[
            pl.BlockSpec((ROWS, D), lambda i: (0, 0)),
            pl.BlockSpec((ROWS, D), lambda i: (0, 0)),
        ],
        out_shape=[
            jax.ShapeDtypeStruct((ROWS, D), F32),
            jax.ShapeDtypeStruct((ROWS, D), BF16),
        ],
        name="after_time",
    )(mixed, patches, w_time, gain)


def spread_matrix():
    i = lax.broadcasted_iota(jnp.int32, (256, 192), 0)
    j = lax.broadcasted_iota(jnp.int32, (256, 192), 1)
    same = (i >> 5) == ((j & 15) >> 1)
    place = (i & 31) == 2 * (j >> 4) + (j & 1)
    return (same & place).astype(F32).astype(BF16)


def gather_matrix():
    j = lax.broadcasted_iota(jnp.int32, (192, 256), 0)
    i = lax.broadcasted_iota(jnp.int32, (192, 256), 1)
    same = (i >> 5) == ((j & 15) >> 1)
    place = (i & 31) == 2 * (j >> 4) + (j & 1)
    return (same & place).astype(F32).astype(BF16)


def unpack(block_ref, rows_ref):
    pick = gather_matrix()
    for j in range(BLOCKS):
        rows_ref[0:256, j * 128 : (j + 1) * 128] = block_ref[
            :, j * 16 : (j + 1) * 16, :
        ].reshape(256, 128)
    for half in range(2):
        packed = block_ref[half * 8 : (half + 1) * 8, 192:224, :].reshape(256, 128)
        last = dot(pick, packed).astype(BF16)
        for j in range(BLOCKS):
            rows_ref[256 + half * 16 : 272 + half * 16, j * 128 : (j + 1) * 128] = last[
                j * 16 : (j + 1) * 16, :
            ]


def space_kernel(
    normed_ref,
    w_ref,
    merge_ref,
    after_ref,
    gain_ref,
    main_ref,
    last_ref,
    space_ref,
    send_ref,
    projected,
    total,
):
    step = pl.program_id(0)

    @pl.when(step < FRAMES)
    def _():
        part = None
        for z in range(4):
            term = dot_nt(w_ref[0, z], normed_ref[:, z * 384 : (z + 1) * 384])
            part = term if part is None else part + term
        projected[pl.ds(pl.multiple_of(step * 288, 32), 288), :] = part.astype(BF16)

    @pl.when(step == FRAMES)
    def _():
        total[...] = after_ref[...]

    @pl.when(step >= FRAMES)
    def _():
        first = pl.multiple_of((step - FRAMES) * 128, 128)
        outs = []
        for head in range(2):
            base = first + head * HEAD
            q = projected[pl.ds(pl.multiple_of(base, 64), HEAD), :]
            k = projected[pl.ds(pl.multiple_of(base + D, 64), HEAD), :]
            v = projected[pl.ds(pl.multiple_of(base + 2 * D, 64), HEAD), :]
            scores = lax.dot_general(
                k, q, (((0,), (0,)), ((), ())), preferred_element_type=F32
            ) * (1.0 / math.sqrt(HEAD))
            powers = jnp.exp(scores - jnp.max(scores, axis=0, keepdims=True))
            weights = (powers * (1.0 / jnp.sum(powers, axis=0, keepdims=True))).astype(BF16)
            outs.append(dot(v, weights))
        both = jnp.concatenate(outs, axis=0).T.astype(BF16)
        total[...] += dot(both, merge_ref[...])

    @pl.when(step == FRAMES + BLOCKS - 1)
    def _():
        after_space = total[...]
        space_ref[...] = after_space
        mixed_in = norm_rows(after_space, gain_ref[...])
        slot = lax.broadcasted_iota(jnp.int32, (512, ROWS), 0)
        chosen = (slot == main_ref[0:1, :]) | (slot == main_ref[1:2, :])
        rows = dot(chosen.astype(F32).astype(BF16), mixed_in).astype(BF16)
        slot = lax.broadcasted_iota(jnp.int32, (64, ROWS), 0)
        chosen = (slot == last_ref[0:1, :]) | (slot == last_ref[1:2, :])
        last = dot(chosen.astype(F32).astype(BF16), mixed_in).astype(BF16)
        for j in range(BLOCKS):
            piece = rows[:, j * 128 : (j + 1) * 128].reshape(EXPERTS, 16, 128)
            for copy in range(2):
                send_ref[:, copy, j * 16 : (j + 1) * 16, :] = piece
        spread = spread_matrix()
        for group in range(4):
            own = last[group * 16 : (group + 1) * 16, :]
            tall = jnp.concatenate(
                [own[:, j * 128 : (j + 1) * 128] for j in range(BLOCKS)], axis=0
            )
            packed = dot(spread, tall).astype(BF16).reshape(8, 32, 128)
            for copy in range(2):
                send_ref[group * 8 : (group + 1) * 8, copy, 192:224, :] = packed


def space_step(normed, w_rows, w_merge, after_time, gain, main, last):
    whole = lambda i: (0, 0)
    return pl.pallas_call(
        space_kernel,
        grid=(FRAMES + BLOCKS,),
        in_specs=[
            pl.BlockSpec((ROWS, D), whole),
            pl.BlockSpec((1, 4, 288, 384), lambda i: (jnp.minimum(i, FRAMES - 1), 0, 0, 0)),
            pl.BlockSpec((128, D), lambda i: (jnp.maximum(i - FRAMES, 0), 0)),
            pl.BlockSpec((ROWS, D), whole),
            pl.BlockSpec((1, D), whole),
            pl.BlockSpec((2, ROWS), whole),
            pl.BlockSpec((2, ROWS), whole),
        ],
        out_specs=[
            pl.BlockSpec((ROWS, D), whole),
            pl.BlockSpec((EXPERTS, 2, PACK, 128), lambda i: (0, 0, 0, 0)),
        ],
        out_shape=[
            jax.ShapeDtypeStruct((ROWS, D), F32),
            jax.ShapeDtypeStruct((EXPERTS, 2, PACK, 128), BF16),
        ],
        scratch_shapes=[pltpu.VMEM((3 * D, ROWS), BF16), pltpu.VMEM((ROWS, D), F32)],
        compiler_params=pltpu.CompilerParams(vmem_limit_bytes=40 * MIB),
        name="space_attention",
    )(normed, w_rows, w_merge, after_time, gain, main, last)


CUT = 256
CUTS = D // CUT


def expert_kernel(with_sum, *refs):
    if with_sum:
        x_ref, other_ref, expand_hbm, reduce_hbm, o_ref = refs[:5]
    else:
        x_ref, expand_hbm, reduce_hbm, o_ref = refs[:4]
    expand, reduce, rows, hidden, sems = refs[-5:]
    step = pl.program_id(0)

    def fetch(n):
        cols = pl.ds((n % CUTS) * CUT, CUT)
        source, target = (expand_hbm, expand) if n < CUTS else (reduce_hbm, reduce)
        return pltpu.make_async_copy(source.at[0, :, cols], target.at[:, cols], sems.at[n])

    @pl.when(step == 0)
    def _():
        for n in range(2 * CUTS):
            fetch(n).start()

    unpack(x_ref, rows)
    for n in range(CUTS):

        @pl.when(step == 0)
        def _():
            fetch(n).wait()

        inner = dot(rows[...], expand[:, n * CUT : (n + 1) * CUT])
        active = inner * (0.5 + 0.5 * lax.erf(inner * math.sqrt(0.5)))
        hidden[:, n * CUT : (n + 1) * CUT] = active.astype(BF16)
    spread = spread_matrix()
    tops = [[], []]
    for n in range(CUTS):

        @pl.when(step == 0)
        def _():
            fetch(CUTS + n).wait()

        part = dot(hidden[...], reduce[:, n * CUT : (n + 1) * CUT])
        for j in range(CUT // 128):
            at = n * (CUT // 128) + j
            piece = part[:, j * 128 : (j + 1) * 128]
            main = piece[0:256].reshape(16, 16, 128)
            if with_sum:
                main = main + other_ref[:, at * 16 : (at + 1) * 16, :].astype(F32)
            o_ref[:, at * 16 : (at + 1) * 16, :] = main.astype(BF16)
            for half in range(2):
                tops[half].append(piece[256 + half * 16 : 272 + half * 16].astype(BF16))
    for half in range(2):
        packed = dot(spread, jnp.concatenate(tops[half], axis=0)).reshape(8, 32, 128)
        if with_sum:
            packed = packed + other_ref[half * 8 : (half + 1) * 8, 192:224, :].astype(F32)
        o_ref[half * 8 : (half + 1) * 8, 192:224, :] = packed.astype(BF16)


def run_experts(first, count, arrived, expand, reduce, other=None):
    block = (16, PACK, 128)
    from_first = pl.BlockSpec(block, lambda i: (i + first, 0, 0))
    from_zero = pl.BlockSpec(block, lambda i: (i, 0, 0))
    anywhere = pl.BlockSpec(memory_space=pl.ANY)
    more = [] if other is None else [other]

    def kernel(*refs):
        expert_kernel(other is not None, *refs)

    return pl.pallas_call(
        kernel,
        grid=(count,),
        in_specs=[from_first] + [from_zero] * len(more) + [anywhere, anywhere],
        out_specs=from_zero,
        out_shape=jax.ShapeDtypeStruct((16 * count, PACK, 128), BF16),
        scratch_shapes=[
            pltpu.VMEM((D, D), BF16),
            pltpu.VMEM((D, D), BF16),
            pltpu.VMEM((288, D), BF16),
            pltpu.VMEM((288, D), BF16),
            pltpu.SemaphoreType.DMA((2 * CUTS,)),
        ],
        compiler_params=pltpu.CompilerParams(vmem_limit_bytes=40 * MIB),
        cost_estimate=pl.CostEstimate(
            flops=count * 288 * D * D * 4,
            bytes_accessed=4 * D * D + count * 32 * PACK * 128 * 2,
            transcendentals=count * 288 * D,
        ),
        name="experts",
    )(arrived, *more, expand, reduce)


def combine_kernel(x_ref, main_ref, last_ref, gate_ref, space_ref, o_ref, rows, totals):
    step = pl.program_id(0)

    @pl.when(step == 0)
    def _():
        totals[...] = jnp.zeros_like(totals)

    unpack(x_ref, rows)
    at = lax.broadcasted_iota(jnp.int32, (ROWS, 288), 1)
    in_last = at >= 256
    expert = jnp.where(in_last, (at - 256) >> 2, at >> 5) + step * 8
    code = jnp.where(in_last, expert * 2 + (at & 1), expert * 16 + (at & 15))
    for k in range(2):
        wanted = jnp.where(in_last, last_ref[:, k : k + 1], main_ref[:, k : k + 1])
        totals[k] += dot((code == wanted).astype(F32).astype(BF16), rows[...])

    @pl.when(step == 3)
    def _():
        mix = totals[0] * gate_ref[:, 0:1] + totals[1] * gate_ref[:, 1:2]
        o_ref[...] = (space_ref[...] + mix).astype(BF16)


def combine(returned, main, last, gates, after_space):
    whole = lambda i: (0, 0)
    return pl.pallas_call(
        combine_kernel,
        grid=(4,),
        in_specs=[
            pl.BlockSpec((16, PACK, 128), lambda i: (i, 0, 0)),
            pl.BlockSpec((ROWS, 2), whole),
            pl.BlockSpec((ROWS, 2), whole),
            pl.BlockSpec((ROWS, 2), whole),
            pl.BlockSpec((ROWS, D), whole),
        ],
        out_specs=pl.BlockSpec((ROWS, D), whole),
        out_shape=jax.ShapeDtypeStruct((ROWS, D), BF16),
        scratch_shapes=[pltpu.VMEM((288, D), BF16), pltpu.VMEM((2, ROWS, D), F32)],
        compiler_params=pltpu.CompilerParams(vmem_limit_bytes=40 * MIB),
        name="combine",
    )(returned, main, last, gates, after_space)


def shards(
    patches,
    temporal_q,
    temporal_k,
    temporal_v,
    clip_lengths,
    w_time,
    gain_space,
    w_space,
    w_merge,
    gain_mix,
    expert_ids,
    gate_weights,
    w_expand,
    w_reduce,
):
    frame_axes, chip_axes = ("x", "y"), ("x", "y", "z")
    swap = [(0, 1), (1, 0)]

    own_rows = lax.dynamic_slice(
        w_space,
        (lax.axis_index("z") * 384, lax.axis_index("c") * 144),
        (384, 144),
    ).T
    w_rows = lax.all_gather(own_rows, ("x", "y", "z", "c"), axis=0, tiled=True)
    w_rows = w_rows.reshape(FRAMES, 4, 288, 384)

    qkv = jnp.concatenate(
        [a.reshape(FRAMES, 16, D) for a in (temporal_q, temporal_k, temporal_v)], axis=1
    )
    qkv = lax.all_to_all(qkv, frame_axes, split_axis=0, concat_axis=0, tiled=True)
    mixed = time_attention(clip_lengths, qkv)
    mixed = lax.all_to_all(mixed, frame_axes, split_axis=0, concat_axis=0, tiled=True)
    after_time, normed = after_time_step(
        mixed.reshape(ROWS, D), patches.reshape(ROWS, D), w_time, gain_space.reshape(1, D)
    )

    experts = expert_ids.reshape(ROWS * 2)
    index = jnp.arange(ROWS * 2, dtype=jnp.int32)
    earlier = (experts[:, None] == experts[None, :]) & (index[None, :] < index[:, None])
    slot = jnp.sum(earlier.astype(jnp.int32), axis=1)
    main = jnp.where(slot < MAIN, experts * MAIN + slot, -1).reshape(ROWS, 2)
    last = jnp.where(slot >= MAIN, experts * 2 + slot - MAIN, -1).reshape(ROWS, 2)

    after_space, outgoing = space_step(
        normed, w_rows, w_merge, after_time, gain_mix.reshape(1, D), main.T, last.T
    )
    arrived = lax.all_to_all(
        outgoing.reshape(64, PACK, 128), chip_axes, split_axis=0, concat_axis=0, tiled=True
    )
    theirs = lax.ppermute(arrived, "c", swap)
    part_own = run_experts(0, 2, arrived, w_expand, w_reduce)
    part_a = run_experts(0, 2, theirs, w_expand, w_reduce)
    back_a = lax.ppermute(part_a, "c", swap)
    part_b = run_experts(2, 2, theirs, w_expand, w_reduce)
    back_b = lax.ppermute(part_b, "c", swap)
    sum_a = (part_own.astype(F32) + back_a.astype(F32)).astype(BF16)
    sum_b = run_experts(2, 2, arrived, w_expand, w_reduce, back_b)
    returned = lax.all_to_all(
        jnp.concatenate([sum_a, sum_b], axis=0), chip_axes, split_axis=0, concat_axis=0, tiled=True
    )
    out = combine(returned, main, last, gate_weights.reshape(ROWS, 2), after_space)
    return out.reshape(patches.shape)


def solution(mesh):
    grid = Mesh(mesh.devices.reshape(4, 4, 4, 2), ("x", "y", "z", "c"))
    frame, clip = ("x", "y"), ("z", "c")
    every = ("x", "y", "z", "c")
    return jax.shard_map(
        shards,
        mesh=grid,
        in_specs=(
            P(frame, clip, None, None),
            P(frame, clip, None, None),
            P(frame, clip, None, None),
            P(frame, clip, None, None),
            P(clip),
            P(),
            P(),
            P(None, frame),
            P(),
            P(),
            P(frame, clip, None, None),
            P(frame, clip, None, None),
            P(every, None, None),
            P(every, None, None),
        ),
        out_specs=P(frame, clip, None, None),
        check_vma=False,
    )
```

```python
import math

import jax
import jax.numpy as jnp
from jax import lax
from jax.experimental import pallas as pl
from jax.experimental.pallas import tpu as pltpu
from jax.sharding import Mesh, PartitionSpec as P

HEADS = 24
HEAD = 64
EXPERTS = 32
D = 1536
ROWS = 256
FRAMES = 16
MAIN = 16
PACK = 224
BLOCKS = D // 128
EPSILON = 1e-06
F32 = jnp.float32
BF16 = jnp.bfloat16
VMEM = 40 << 20


def dot(a, b):
    return jnp.dot(a, b, preferred_element_type=F32)


def dot_nt(a, b):
    return lax.dot_general(a, b, (((1,), (1,)), ((), ())), preferred_element_type=F32)


def in_vmem(array):
    return pltpu.with_memory_space_constraint(array, pltpu.VMEM)


def in_hbm(array):
    return pltpu.with_memory_space_constraint(array, pltpu.HBM)


def norm_rows(values, gain):
    centre = values - jnp.mean(values, axis=-1, keepdims=True)
    spread = jnp.mean(centre * centre, axis=-1, keepdims=True)
    return (centre * lax.rsqrt(spread + EPSILON) * gain).astype(BF16)


TIME_PAIRS = 3


def time_kernel(len_ref, x_ref, o_ref):
    row = lax.broadcasted_iota(jnp.int32, (ROWS, ROWS), 0)
    col = lax.broadcasted_iota(jnp.int32, (ROWS, ROWS), 1)
    keep = ((row & 15) == (col & 15)) & ((col >> 4) < len_ref[0])
    low = lax.broadcasted_iota(jnp.int32, (ROWS, 128), 1) < HEAD
    zero = jnp.zeros((ROWS, 128), BF16)
    def heads(step, carry):
        for pair in range(TIME_PAIRS):
            lanes = pl.ds(pl.multiple_of((step * TIME_PAIRS + pair) * 128, 128), 128)
            q = x_ref[:, 0:16, lanes].reshape(ROWS, 128)
            k = x_ref[:, 16:32, lanes].reshape(ROWS, 128)
            v = x_ref[:, 32:48, lanes].reshape(ROWS, 128)
            total = None
            for head in range(2):
                mine = low if head == 0 else ~low
                scores = dot_nt(q, jnp.where(mine, k, zero)) * (1.0 / math.sqrt(HEAD))
                scores = jnp.where(keep, scores, -1e30)
                powers = jnp.exp(scores - jnp.max(scores, axis=-1, keepdims=True))
                weights = (powers * (1.0 / jnp.sum(powers, axis=-1, keepdims=True))).astype(BF16)
                part = dot(weights, jnp.where(mine, v, zero))
                total = part if total is None else total + part
            o_ref[:, :, lanes] = total.astype(BF16).reshape(FRAMES, 16, 128)
        return carry

    lax.fori_loop(0, BLOCKS // TIME_PAIRS, heads, 0)


def time_attention(lengths, qkv):
    return pl.pallas_call(
        time_kernel,
        in_specs=[
            pl.BlockSpec(memory_space=pltpu.SMEM),
            pl.BlockSpec(memory_space=pltpu.VMEM),
        ],
        out_shape=jax.ShapeDtypeStruct((FRAMES, 16, D), BF16),
        compiler_params=pltpu.CompilerParams(vmem_limit_bytes=16 << 20),
        name="time_attention",
    )(lengths, in_vmem(qkv))


def after_time_kernel(mixed_ref, patch_ref, w_ref, gain_ref, after_ref, normed_ref):
    after_time = patch_ref[...].astype(F32) + dot(mixed_ref[...], w_ref[...])
    after_ref[...] = after_time
    normed_ref[...] = norm_rows(after_time, gain_ref[...])


def after_time_step(mixed, patches, w_time, gain):
    return pl.pallas_call(
        after_time_kernel,
        out_shape=[
            jax.ShapeDtypeStruct((ROWS, D), F32),
            jax.ShapeDtypeStruct((ROWS, D), BF16),
        ],
        compiler_params=pltpu.CompilerParams(vmem_limit_bytes=24 << 20),
        name="after_time",
    )(mixed, patches, in_hbm(w_time), gain)


def spread_matrix():
    i = lax.broadcasted_iota(jnp.int32, (256, 192), 0)
    j = lax.broadcasted_iota(jnp.int32, (256, 192), 1)
    same = (i >> 5) == ((j & 15) >> 1)
    place = (i & 31) == 2 * (j >> 4) + (j & 1)
    return (same & place).astype(F32).astype(BF16)


def gather_matrix():
    j = lax.broadcasted_iota(jnp.int32, (192, 256), 0)
    i = lax.broadcasted_iota(jnp.int32, (192, 256), 1)
    same = (i >> 5) == ((j & 15) >> 1)
    place = (i & 31) == 2 * (j >> 4) + (j & 1)
    return (same & place).astype(F32).astype(BF16)


def unpack(block_ref, rows_ref, chunks):
    pick = gather_matrix()
    whole = chunks * 16
    for j in range(BLOCKS):
        rows_ref[0:whole, j * 128 : (j + 1) * 128] = block_ref[
            :, j * 16 : (j + 1) * 16, :
        ].reshape(whole, 128)
    for group in range(chunks // 8):
        packed = block_ref[group * 8 : (group + 1) * 8, 192:224, :].reshape(256, 128)
        last = dot(pick, packed).astype(BF16)
        at = whole + group * 16
        for j in range(BLOCKS):
            rows_ref[at : at + 16, j * 128 : (j + 1) * 128] = last[j * 16 : (j + 1) * 16, :]


GROUPS = 4
PAIRS = 2


def space_kernel(
    normed_ref,
    w_hbm,
    merge_hbm,
    after_ref,
    gain_ref,
    main_ref,
    last_ref,
    space_ref,
    send_ref,
    w_rows,
    merge,
    projected,
    spatial,
    sems,
):
    per_group = FRAMES // GROUPS
    high = per_group * 288

    def fetch(group, frame, z):
        f = group * per_group + frame
        return pltpu.make_async_copy(
            w_hbm.at[f, z],
            w_rows.at[pl.ds(f * 288, 288), pl.ds(z * 384, 384)],
            sems.at[group],
        )

    every = [(frame, z) for frame in range(per_group) for z in range(4)]
    for group in range(GROUPS):
        for frame, z in every:
            fetch(group, frame, z).start()
    fetch_merge = pltpu.make_async_copy(merge_hbm, merge, sems.at[GROUPS])
    fetch_merge.start()
    for group in range(GROUPS):
        for frame, z in every:
            fetch(group, frame, z).wait()
        rows = slice(group * high, (group + 1) * high)
        projected[:, rows] = dot_nt(normed_ref[...], w_rows[rows, :]).astype(BF16)

    low = lax.broadcasted_iota(jnp.int32, (ROWS, 128), 1) < HEAD
    zero = jnp.zeros((ROWS, 128), BF16)

    def heads(step, carry):
        for pair in range(PAIRS):
            first = pl.multiple_of((step * PAIRS + pair) * 128, 128)
            q = projected[:, pl.ds(first, 128)]
            k = projected[:, pl.ds(pl.multiple_of(first + D, 128), 128)]
            v = projected[:, pl.ds(pl.multiple_of(first + 2 * D, 128), 128)]
            mixed = None
            for head in range(2):
                mine = low if head == 0 else ~low
                scores = dot_nt(q, jnp.where(mine, k, zero)) * (1.0 / math.sqrt(HEAD))
                powers = jnp.exp(scores - jnp.max(scores, axis=-1, keepdims=True))
                weights = (powers * (1.0 / jnp.sum(powers, axis=-1, keepdims=True))).astype(BF16)
                part = dot(weights, jnp.where(mine, v, zero))
                mixed = part if mixed is None else mixed + part
            spatial[:, pl.ds(first, 128)] = mixed.astype(BF16)
        return carry

    lax.fori_loop(0, BLOCKS // PAIRS, heads, 0)
    fetch_merge.wait()
    after_space = after_ref[...] + dot(spatial[...], merge[...])
    space_ref[...] = after_space
    mixed_in = norm_rows(after_space, gain_ref[...])
    slot = lax.broadcasted_iota(jnp.int32, (512, ROWS), 0)
    chosen = (slot == main_ref[0:1, :]) | (slot == main_ref[1:2, :])
    rows = dot(chosen.astype(F32).astype(BF16), mixed_in).astype(BF16)
    slot = lax.broadcasted_iota(jnp.int32, (64, ROWS), 0)
    chosen = (slot == last_ref[0:1, :]) | (slot == last_ref[1:2, :])
    last = dot(chosen.astype(F32).astype(BF16), mixed_in).astype(BF16)
    for j in range(BLOCKS):
        piece = rows[:, j * 128 : (j + 1) * 128].reshape(EXPERTS, 16, 128)
        for copy in range(2):
            send_ref[:, copy, j * 16 : (j + 1) * 16, :] = piece
    spread = spread_matrix()
    for group in range(4):
        own = last[group * 16 : (group + 1) * 16, :]
        tall = jnp.concatenate([own[:, j * 128 : (j + 1) * 128] for j in range(BLOCKS)], axis=0)
        packed = dot(spread, tall).astype(BF16).reshape(8, 32, 128)
        for copy in range(2):
            send_ref[group * 8 : (group + 1) * 8, copy, 192:224, :] = packed


def space_step(normed, w_rows, w_merge, after_time, gain, main, last):
    whole = lambda i: (0, 0)
    anywhere = pl.BlockSpec(memory_space=pl.ANY)
    return pl.pallas_call(
        space_kernel,
        grid=(1,),
        in_specs=[
            pl.BlockSpec((ROWS, D), whole),
            anywhere,
            anywhere,
            pl.BlockSpec((ROWS, D), whole),
            pl.BlockSpec((1, D), whole),
            pl.BlockSpec((2, ROWS), whole),
            pl.BlockSpec((2, ROWS), whole),
        ],
        out_specs=[
            pl.BlockSpec((ROWS, D), whole),
            pl.BlockSpec((EXPERTS, 2, PACK, 128), lambda i: (0, 0, 0, 0)),
        ],
        out_shape=[
            jax.ShapeDtypeStruct((ROWS, D), F32),
            jax.ShapeDtypeStruct((EXPERTS, 2, PACK, 128), BF16),
        ],
        scratch_shapes=[
            pltpu.VMEM((3 * D, D), BF16),
            pltpu.VMEM((D, D), BF16),
            pltpu.VMEM((ROWS, 3 * D), BF16),
            pltpu.VMEM((ROWS, D), BF16),
            pltpu.SemaphoreType.DMA((GROUPS + 1,)),
        ],
        compiler_params=pltpu.CompilerParams(vmem_limit_bytes=VMEM),
        name="space_attention",
    )(normed, w_rows, in_hbm(w_merge), after_time, gain, main, last)


CHUNKS = 32
EXPERT_ROWS = CHUNKS * 18
CUT = 512
CUTS = D // CUT


def first_kernel(x_ref, expand_hbm, reduce_hbm, o_ref, expand, reduce, rows, hidden, sems):
    def fetch(n):
        cols = pl.ds((n % CUTS) * CUT, CUT)
        source, target = (expand_hbm, expand) if n < CUTS else (reduce_hbm, reduce)
        return pltpu.make_async_copy(source.at[:, :, cols], target.at[:, :, cols], sems.at[n])

    for n in range(2 * CUTS):
        fetch(n).start()
    expert_body(x_ref, expand, reduce, o_ref, rows, hidden, lambda n: fetch(n).wait())


def later_kernel(x_ref, expand, reduce, o_ref, rows, hidden):
    expert_body(x_ref, expand, reduce, o_ref, rows, hidden, lambda n: None)


def add_kernel(own_a, back_a, own_b, back_b, o_ref):
    step = pl.program_id(0)

    @pl.when(step < 2)
    def _():
        o_ref[...] = (own_a[...].astype(F32) + back_a[...].astype(F32)).astype(BF16)

    @pl.when(step >= 2)
    def _():
        o_ref[...] = (own_b[...].astype(F32) + back_b[...].astype(F32)).astype(BF16)


def add_parts(own_a, back_a, own_b, back_b):
    block = (CHUNKS // 2, PACK, 128)
    first = pl.BlockSpec(block, lambda i: (jnp.minimum(i, 1), 0, 0))
    second = pl.BlockSpec(block, lambda i: (jnp.maximum(i - 2, 0), 0, 0))
    return pl.pallas_call(
        add_kernel,
        grid=(4,),
        in_specs=[first, first, second, second],
        out_specs=pl.BlockSpec(block, lambda i: (i, 0, 0)),
        out_shape=pltpu.HBM((2 * CHUNKS, PACK, 128), BF16),
        compiler_params=pltpu.CompilerParams(vmem_limit_bytes=16 << 20),
        name="add_parts",
    )(own_a, back_a, own_b, back_b)


def expert_body(x_ref, expand, reduce, o_ref, rows, hidden, ready):
    whole = CHUNKS * 16
    unpack(x_ref, rows, CHUNKS)
    for n in range(CUTS):
        ready(n)
        inner = dot(rows[...], expand[0, :, n * CUT : (n + 1) * CUT])
        active = inner * (0.5 + 0.5 * lax.erf(inner * math.sqrt(0.5)))
        hidden[:, n * CUT : (n + 1) * CUT] = active.astype(BF16)
    spread = spread_matrix()
    tops = [[] for _ in range(CHUNKS // 8)]
    for n in range(CUTS):
        ready(CUTS + n)
        part = dot(hidden[...], reduce[0, :, n * CUT : (n + 1) * CUT])
        for j in range(CUT // 128):
            at = n * (CUT // 128) + j
            piece = part[:, j * 128 : (j + 1) * 128]
            main = piece[0:whole].reshape(CHUNKS, 16, 128)
            o_ref[:, at * 16 : (at + 1) * 16, :] = main.astype(BF16)
            for group in range(CHUNKS // 8):
                start = whole + group * 16
                tops[group].append(piece[start : start + 16].astype(BF16))
    for group in range(CHUNKS // 8):
        packed = dot(spread, jnp.concatenate(tops[group], axis=0)).reshape(8, 32, 128)
        at = group * 8
        o_ref[at : at + 8, 192:224, :] = packed.astype(BF16)


EXPERT_SCRATCH = [
    pltpu.VMEM((EXPERT_ROWS, D), BF16),
    pltpu.VMEM((EXPERT_ROWS, D), BF16),
]
EXPERT_COST = pl.CostEstimate(
    flops=EXPERT_ROWS * D * D * 4,
    bytes_accessed=2 * CHUNKS * PACK * 128 * 2,
    transcendentals=EXPERT_ROWS * D,
)
HALF = (CHUNKS, PACK, 128)


def first_experts(arrived, expand, reduce):
    anywhere = pl.BlockSpec(memory_space=pl.ANY)
    resident = pl.BlockSpec(memory_space=pltpu.VMEM)
    return pl.pallas_call(
        first_kernel,
        grid=(1,),
        in_specs=[pl.BlockSpec(HALF, lambda i: (0, 0, 0)), anywhere, anywhere],
        out_specs=[pl.BlockSpec(HALF, lambda i: (0, 0, 0)), resident, resident],
        out_shape=[
            jax.ShapeDtypeStruct(HALF, BF16),
            pltpu.VMEM((1, D, D), BF16),
            pltpu.VMEM((1, D, D), BF16),
        ],
        scratch_shapes=EXPERT_SCRATCH + [pltpu.SemaphoreType.DMA((2 * CUTS,))],
        compiler_params=pltpu.CompilerParams(vmem_limit_bytes=18 << 20),
        cost_estimate=EXPERT_COST,
        name="experts",
    )(arrived, in_hbm(expand), in_hbm(reduce))


def run_experts(half, arrived, expand, reduce):
    resident = pl.BlockSpec(memory_space=pltpu.VMEM)
    return pl.pallas_call(
        later_kernel,
        grid=(1,),
        in_specs=[pl.BlockSpec(HALF, lambda i: (half, 0, 0)), resident, resident],
        out_specs=pl.BlockSpec(HALF, lambda i: (0, 0, 0)),
        out_shape=jax.ShapeDtypeStruct(HALF, BF16),
        scratch_shapes=EXPERT_SCRATCH,
        compiler_params=pltpu.CompilerParams(vmem_limit_bytes=18 << 20),
        cost_estimate=EXPERT_COST,
        name="experts",
    )(arrived, in_vmem(expand), in_vmem(reduce))


def combine_kernel(x_ref, main_ref, last_ref, gate_ref, space_ref, o_ref, rows, totals):
    step = pl.program_id(0)

    @pl.when(step == 0)
    def _():
        totals[...] = jnp.zeros_like(totals)

    unpack(x_ref, rows, 16)
    at = lax.broadcasted_iota(jnp.int32, (ROWS, 288), 1)
    in_last = at >= 256
    expert = jnp.where(in_last, (at - 256) >> 2, at >> 5) + step * 8
    code = jnp.where(in_last, expert * 2 + (at & 1), expert * 16 + (at & 15))
    for k in range(2):
        wanted = jnp.where(in_last, last_ref[:, k : k + 1], main_ref[:, k : k + 1])
        totals[k] += dot((code == wanted).astype(F32).astype(BF16), rows[...])

    @pl.when(step == 3)
    def _():
        mix = totals[0] * gate_ref[:, 0:1] + totals[1] * gate_ref[:, 1:2]
        o_ref[...] = (space_ref[...] + mix).astype(BF16)


def combine(returned, main, last, gates, after_space):
    whole = lambda i: (0, 0)
    return pl.pallas_call(
        combine_kernel,
        grid=(4,),
        in_specs=[
            pl.BlockSpec((16, PACK, 128), lambda i: (i, 0, 0)),
            pl.BlockSpec((ROWS, 2), whole),
            pl.BlockSpec((ROWS, 2), whole),
            pl.BlockSpec((ROWS, 2), whole),
            pl.BlockSpec((ROWS, D), whole),
        ],
        out_specs=pl.BlockSpec((ROWS, D), whole),
        out_shape=jax.ShapeDtypeStruct((ROWS, D), BF16),
        scratch_shapes=[pltpu.VMEM((288, D), BF16), pltpu.VMEM((2, ROWS, D), F32)],
        compiler_params=pltpu.CompilerParams(vmem_limit_bytes=VMEM),
        name="combine",
    )(returned, main, last, gates, after_space)


def shards(
    patches,
    temporal_q,
    temporal_k,
    temporal_v,
    clip_lengths,
    w_time,
    gain_space,
    w_space,
    w_merge,
    gain_mix,
    expert_ids,
    gate_weights,
    w_expand,
    w_reduce,
):
    frame_axes, chip_axes = ("x", "y"), ("x", "y", "z")
    swap = [(0, 1), (1, 0)]

    own_rows = lax.dynamic_slice(
        w_space,
        (lax.axis_index("z") * 384, lax.axis_index("c") * 144),
        (384, 144),
    ).T
    w_rows = lax.all_gather(own_rows, ("x", "y", "z", "c"), axis=0, tiled=True)
    w_rows = w_rows.reshape(FRAMES, 4, 288, 384)

    qkv_own = jnp.concatenate(
        [a.reshape(FRAMES, 16, D) for a in (temporal_q, temporal_k, temporal_v)], axis=1
    )
    qkv = lax.all_to_all(qkv_own, frame_axes, split_axis=0, concat_axis=0, tiled=True)
    mixed = time_attention(clip_lengths, qkv)
    mixed = lax.all_to_all(mixed, frame_axes, split_axis=0, concat_axis=0, tiled=True)
    after_time, normed = after_time_step(
        mixed.reshape(ROWS, D), patches.reshape(ROWS, D), w_time, gain_space.reshape(1, D)
    )

    experts = expert_ids.reshape(ROWS * 2)
    index = jnp.arange(ROWS * 2, dtype=jnp.int32)
    earlier = (experts[:, None] == experts[None, :]) & (index[None, :] < index[:, None])
    slot = jnp.sum(earlier.astype(jnp.int32), axis=1)
    main = jnp.where(slot < MAIN, experts * MAIN + slot, -1).reshape(ROWS, 2)
    last = jnp.where(slot >= MAIN, experts * 2 + slot - MAIN, -1).reshape(ROWS, 2)

    after_space, outgoing = space_step(
        normed, w_rows, w_merge, after_time, gain_mix.reshape(1, D), main.T, last.T
    )
    arrived = lax.all_to_all(
        outgoing.reshape(64, PACK, 128), chip_axes, split_axis=0, concat_axis=0, tiled=True
    )
    theirs = lax.ppermute(arrived, "c", swap)
    part_own, expand, reduce = first_experts(arrived, w_expand, w_reduce)
    theirs, part_own = lax.optimization_barrier((theirs, part_own))
    part_a = run_experts(0, theirs, expand, reduce)
    back_a = lax.ppermute(part_a, "c", swap)
    part_b = run_experts(1, theirs, expand, reduce)
    back_b = lax.ppermute(part_b, "c", swap)
    part_own_b = run_experts(1, arrived, expand, reduce)
    sums = add_parts(part_own, back_a, part_own_b, back_b)
    returned = lax.all_to_all(sums, chip_axes, split_axis=0, concat_axis=0, tiled=True)
    out = combine(returned, main, last, gate_weights.reshape(ROWS, 2), after_space)
    return out.reshape(patches.shape)


def solution(mesh):
    grid = Mesh(mesh.devices.reshape(4, 4, 4, 2), ("x", "y", "z", "c"))
    frame, clip = ("x", "y"), ("z", "c")
    every = ("x", "y", "z", "c")
    return jax.shard_map(
        shards,
        mesh=grid,
        in_specs=(
            P(frame, clip, None, None),
            P(frame, clip, None, None),
            P(frame, clip, None, None),
            P(frame, clip, None, None),
            P(clip),
            P(),
            P(),
            P(None, frame),
            P(),
            P(),
            P(frame, clip, None, None),
            P(frame, clip, None, None),
            P(every, None, None),
            P(every, None, None),
        ),
        out_specs=P(frame, clip, None, None),
        check_vma=False,
    )
```

```python
import math

import jax
import jax.numpy as jnp
from jax import lax
from jax.experimental import pallas as pl
from jax.experimental.pallas import tpu as pltpu
from jax.sharding import Mesh, PartitionSpec as P

HEADS = 24
HEAD = 64
EXPERTS = 32
D = 1536
ROWS = 256
FRAMES = 16
MAIN = 16
PACKS = (96, 128)
CHIPS = 64
BLOCKS = D // 128
EPSILON = 1e-06
F32 = jnp.float32
BF16 = jnp.bfloat16
VMEM = 40 << 20


def dot(a, b):
    return jnp.dot(a, b, preferred_element_type=F32)


def dot_nt(a, b):
    return lax.dot_general(a, b, (((1,), (1,)), ((), ())), preferred_element_type=F32)


def in_vmem(array):
    return pltpu.with_memory_space_constraint(array, pltpu.VMEM)


def in_hbm(array):
    return pltpu.with_memory_space_constraint(array, pltpu.HBM)


def norm_rows(values, gain):
    centre = values - jnp.mean(values, axis=-1, keepdims=True)
    spread = jnp.mean(centre * centre, axis=-1, keepdims=True)
    return (centre * lax.rsqrt(spread + EPSILON) * gain).astype(BF16)


TIME_PAIRS = 3


def time_kernel(len_ref, x_ref, o_ref):
    row = lax.broadcasted_iota(jnp.int32, (ROWS, ROWS), 0)
    col = lax.broadcasted_iota(jnp.int32, (ROWS, ROWS), 1)
    keep = ((row & 15) == (col & 15)) & ((col >> 4) < len_ref[0])
    low = lax.broadcasted_iota(jnp.int32, (ROWS, 128), 1) < HEAD
    zero = jnp.zeros((ROWS, 128), BF16)
    def heads(step, carry):
        for pair in range(TIME_PAIRS):
            lanes = pl.ds(pl.multiple_of((step * TIME_PAIRS + pair) * 128, 128), 128)
            q = x_ref[:, 0:16, lanes].reshape(ROWS, 128)
            k = x_ref[:, 16:32, lanes].reshape(ROWS, 128)
            v = x_ref[:, 32:48, lanes].reshape(ROWS, 128)
            total = None
            for head in range(2):
                mine = low if head == 0 else ~low
                scores = dot_nt(q, jnp.where(mine, k, zero)) * (1.0 / math.sqrt(HEAD))
                scores = jnp.where(keep, scores, -1e30)
                powers = jnp.exp(scores - jnp.max(scores, axis=-1, keepdims=True))
                weights = (powers * (1.0 / jnp.sum(powers, axis=-1, keepdims=True))).astype(BF16)
                part = dot(weights, jnp.where(mine, v, zero))
                total = part if total is None else total + part
            o_ref[:, :, lanes] = total.astype(BF16).reshape(FRAMES, 16, 128)
        return carry

    lax.fori_loop(0, BLOCKS // TIME_PAIRS, heads, 0)


def time_attention(lengths, qkv):
    return pl.pallas_call(
        time_kernel,
        in_specs=[
            pl.BlockSpec(memory_space=pltpu.SMEM),
            pl.BlockSpec(memory_space=pltpu.VMEM),
        ],
        out_shape=jax.ShapeDtypeStruct((FRAMES, 16, D), BF16),
        compiler_params=pltpu.CompilerParams(vmem_limit_bytes=16 << 20),
        name="time_attention",
    )(lengths, in_vmem(qkv))


def after_time_kernel(mixed_ref, patch_ref, w_ref, gain_ref, after_ref, normed_ref):
    after_time = patch_ref[...].astype(F32) + dot(mixed_ref[...], w_ref[...])
    after_ref[...] = after_time
    normed_ref[...] = norm_rows(after_time, gain_ref[...])


def after_time_step(mixed, patches, w_time, gain):
    return pl.pallas_call(
        after_time_kernel,
        out_shape=[
            jax.ShapeDtypeStruct((ROWS, D), F32),
            jax.ShapeDtypeStruct((ROWS, D), BF16),
        ],
        compiler_params=pltpu.CompilerParams(vmem_limit_bytes=24 << 20),
        name="after_time",
    )(mixed, patches, in_hbm(w_time), gain)


def spread_matrix():
    i = lax.broadcasted_iota(jnp.int32, (256, 192), 0)
    j = lax.broadcasted_iota(jnp.int32, (256, 192), 1)
    same = (i >> 5) == ((j & 15) >> 1)
    place = (i & 31) == 2 * (j >> 4) + (j & 1)
    return (same & place).astype(F32).astype(BF16)


def gather_matrix():
    j = lax.broadcasted_iota(jnp.int32, (192, 256), 0)
    i = lax.broadcasted_iota(jnp.int32, (192, 256), 1)
    same = (i >> 5) == ((j & 15) >> 1)
    place = (i & 31) == 2 * (j >> 4) + (j & 1)
    return (same & place).astype(F32).astype(BF16)


def unpack(block_ref, rows_ref, extra, base=0):
    whole = CHIPS * 8
    for t in range(BLOCKS // 2):
        both = block_ref[:, t * 16 : (t + 1) * 16, :].astype(F32)
        for side in range(2):
            part = both[:, side * 8 : (side + 1) * 8, :].reshape(whole, 128)
            at = (2 * t + side) * 128
            rows_ref[base : base + whole, at : at + 128] = part.astype(BF16)
    if not extra:
        return
    pick = gather_matrix()
    for group in range(CHIPS // 8):
        packed = block_ref[group * 8 : (group + 1) * 8, 96:128, :].reshape(256, 128)
        last = dot(pick, packed).astype(BF16)
        at = base + whole + group * 16
        for j in range(BLOCKS):
            rows_ref[at : at + 16, j * 128 : (j + 1) * 128] = last[j * 16 : (j + 1) * 16, :]


def side_by_side(left, right):
    shape = (left.shape[0] // 8, 8, 128)
    return jnp.concatenate([left.reshape(shape), right.reshape(shape)], axis=1).astype(BF16)


GROUPS = 4
PAIRS = 2


def space_kernel(
    normed_ref,
    w_hbm,
    merge_hbm,
    after_ref,
    gain_ref,
    main_ref,
    last_ref,
    space_ref,
    send_a,
    send_b,
    w_rows,
    merge,
    projected,
    spatial,
    sems,
):
    per_group = FRAMES // GROUPS
    high = per_group * 288

    def fetch(group, frame, z):
        f = group * per_group + frame
        return pltpu.make_async_copy(
            w_hbm.at[f, z],
            w_rows.at[pl.ds(f * 288, 288), pl.ds(z * 384, 384)],
            sems.at[group],
        )

    every = [(frame, z) for frame in range(per_group) for z in range(4)]
    for group in range(GROUPS):
        for frame, z in every:
            fetch(group, frame, z).start()
    fetch_merge = pltpu.make_async_copy(merge_hbm, merge, sems.at[GROUPS])
    fetch_merge.start()
    for group in range(GROUPS):
        for frame, z in every:
            fetch(group, frame, z).wait()
        rows = slice(group * high, (group + 1) * high)
        projected[:, rows] = dot_nt(normed_ref[...], w_rows[rows, :]).astype(BF16)

    low = lax.broadcasted_iota(jnp.int32, (ROWS, 128), 1) < HEAD
    zero = jnp.zeros((ROWS, 128), BF16)

    def heads(step, carry):
        for pair in range(PAIRS):
            first = pl.multiple_of((step * PAIRS + pair) * 128, 128)
            q = projected[:, pl.ds(first, 128)]
            k = projected[:, pl.ds(pl.multiple_of(first + D, 128), 128)]
            v = projected[:, pl.ds(pl.multiple_of(first + 2 * D, 128), 128)]
            mixed = None
            for head in range(2):
                mine = low if head == 0 else ~low
                scores = dot_nt(q, jnp.where(mine, k, zero)) * (1.0 / math.sqrt(HEAD))
                powers = jnp.exp(scores - jnp.max(scores, axis=-1, keepdims=True))
                weights = (powers * (1.0 / jnp.sum(powers, axis=-1, keepdims=True))).astype(BF16)
                part = dot(weights, jnp.where(mine, v, zero))
                mixed = part if mixed is None else mixed + part
            spatial[:, pl.ds(first, 128)] = mixed.astype(BF16)
        return carry

    lax.fori_loop(0, BLOCKS // PAIRS, heads, 0)
    fetch_merge.wait()
    after_space = after_ref[...] + dot(spatial[...], merge[...])
    space_ref[...] = after_space
    mixed_in = norm_rows(after_space, gain_ref[...])
    slot = lax.broadcasted_iota(jnp.int32, (512, ROWS), 0)
    chosen = (slot == main_ref[0:1, :]) | (slot == main_ref[1:2, :])
    rows = dot(chosen.astype(F32).astype(BF16), mixed_in)
    slot = lax.broadcasted_iota(jnp.int32, (64, ROWS), 0)
    chosen = (slot == last_ref[0:1, :]) | (slot == last_ref[1:2, :])
    last = dot(chosen.astype(F32).astype(BF16), mixed_in).astype(BF16)
    for send_ref, own in ((send_a, rows[0:256]), (send_b, rows[256:512])):
        for t in range(BLOCKS // 2):
            at = t * 256
            piece = side_by_side(own[:, at : at + 128], own[:, at + 128 : at + 256])
            for copy in range(2):
                send_ref[:, copy, t * 16 : (t + 1) * 16, :] = piece
    spread = spread_matrix()
    for group in range(4):
        own = last[group * 16 : (group + 1) * 16, :]
        tall = jnp.concatenate([own[:, j * 128 : (j + 1) * 128] for j in range(BLOCKS)], axis=0)
        packed = dot(spread, tall).astype(BF16).reshape(8, 32, 128)
        for copy in range(2):
            send_b[group * 8 : (group + 1) * 8, copy, 96:128, :] = packed


def space_step(normed, w_rows, w_merge, after_time, gain, main, last):
    whole = lambda i: (0, 0)
    anywhere = pl.BlockSpec(memory_space=pl.ANY)
    return pl.pallas_call(
        space_kernel,
        grid=(1,),
        in_specs=[
            pl.BlockSpec((ROWS, D), whole),
            anywhere,
            anywhere,
            pl.BlockSpec((ROWS, D), whole),
            pl.BlockSpec((1, D), whole),
            pl.BlockSpec((2, ROWS), whole),
            pl.BlockSpec((2, ROWS), whole),
        ],
        out_specs=[
            pl.BlockSpec((ROWS, D), whole),
            *(pl.BlockSpec((EXPERTS, 2, pack, 128), lambda i: (0, 0, 0, 0)) for pack in PACKS),
        ],
        out_shape=[
            pltpu.HBM((ROWS, D), F32),
            *(pltpu.HBM((EXPERTS, 2, pack, 128), BF16) for pack in PACKS),
        ],
        scratch_shapes=[
            pltpu.VMEM((3 * D, D), BF16),
            pltpu.VMEM((D, D), BF16),
            pltpu.VMEM((ROWS, 3 * D), BF16),
            pltpu.VMEM((ROWS, D), BF16),
            pltpu.SemaphoreType.DMA((GROUPS + 1,)),
        ],
        compiler_params=pltpu.CompilerParams(vmem_limit_bytes=VMEM),
        name="space_attention",
    )(normed, w_rows, in_hbm(w_merge), after_time, gain, main, last)


CUT = 512
CUTS = D // CUT


def expert_kernel(
    x_ref, y_ref, expand_hbm, reduce_hbm, x_out, y_low, y_high, expand, reduce, rows, hidden, sems
):
    whole = CHIPS * 8
    each = rows.shape[0] // 2
    extra = each > whole

    def fetch(n):
        cols = pl.ds((n % CUTS) * CUT, CUT)
        source, target = (expand_hbm, expand) if n < CUTS else (reduce_hbm, reduce)
        return pltpu.make_async_copy(source.at[0, :, cols], target.at[:, cols], sems.at[n])

    for n in range(2 * CUTS):
        fetch(n).start()
    unpack(x_ref, rows, extra)
    unpack(y_ref, rows, extra, each)
    for n in range(CUTS):
        fetch(n).wait()
        inner = dot(rows[...], expand[:, n * CUT : (n + 1) * CUT])
        active = inner * (0.5 + 0.5 * lax.erf(inner * math.sqrt(0.5)))
        hidden[:, n * CUT : (n + 1) * CUT] = active.astype(BF16)
    tops = [[[] for _ in range(CHIPS // 8)] for _ in range(2)]
    for n in range(CUTS):
        fetch(CUTS + n).wait()
        both = dot(hidden[...], reduce[:, n * CUT : (n + 1) * CUT])
        for side in range(2):
            part = both[side * each : (side + 1) * each]
            for j in range(0, CUT // 128, 2):
                t = (n * (CUT // 128) + j) // 2
                at = j * 128
                tile = slice(t * 16, (t + 1) * 16)
                packed = side_by_side(
                    part[0:whole, at : at + 128], part[0:whole, at + 128 : at + 256]
                )
                if side == 0:
                    x_out[:, tile, :] = packed
                else:
                    y_low[:, tile, :] = packed[0 : CHIPS // 2]
                    y_high[:, tile, :] = packed[CHIPS // 2 :]
            if extra:
                for group in range(CHIPS // 8):
                    start = whole + group * 16
                    for j in range(CUT // 128):
                        piece = part[start : start + 16, j * 128 : (j + 1) * 128]
                        tops[side][group].append(piece.astype(BF16))
    if extra:
        spread = spread_matrix()
        for side in range(2):
            for group in range(CHIPS // 8):
                tall = jnp.concatenate(tops[side][group], axis=0)
                packed = dot(spread, tall).reshape(8, 32, 128).astype(BF16)
                if side == 0:
                    x_out[group * 8 : (group + 1) * 8, 96:128, :] = packed
                else:
                    o_ref = (y_low, y_high)[group // 4]
                    o_ref[(group % 4) * 8 : (group % 4 + 1) * 8, 96:128, :] = packed


SMALL = pl.CostEstimate(flops=1, bytes_accessed=1, transcendentals=0)


def run_experts(own, theirs, expand, reduce):
    shape = own.shape
    count = CHIPS * (8 if shape[1] == PACKS[0] else 10)
    anywhere = pl.BlockSpec(memory_space=pl.ANY)
    return pl.pallas_call(
        expert_kernel,
        in_specs=[pl.BlockSpec(), pl.BlockSpec(), anywhere, anywhere],
        out_shape=[jax.ShapeDtypeStruct(shape, BF16)]
        + [jax.ShapeDtypeStruct((CHIPS // 2, *shape[1:]), BF16)] * 2,
        scratch_shapes=[
            pltpu.VMEM((D, D), BF16),
            pltpu.VMEM((D, D), BF16),
            pltpu.VMEM((2 * count, D), BF16),
            pltpu.VMEM((2 * count, D), BF16),
            pltpu.SemaphoreType.DMA((2 * CUTS,)),
        ],
        compiler_params=pltpu.CompilerParams(vmem_limit_bytes=44 << 20),
        cost_estimate=SMALL,
        name="experts",
    )(own, theirs, in_hbm(expand), in_hbm(reduce))


def add_kernel(own_ref, low_ref, high_ref, o_ref):
    step = pl.program_id(0)
    for back_ref, mine in ((low_ref, step < 2), (high_ref, step >= 2)):

        @pl.when(mine)
        def _():
            o_ref[...] = (own_ref[...].astype(F32) + back_ref[...].astype(F32)).astype(BF16)


def add_parts(own, low, high):
    block = (CHIPS // 4, own.shape[1], 128)
    spec = pl.BlockSpec(block, lambda i: (i, 0, 0))
    return pl.pallas_call(
        add_kernel,
        grid=(4,),
        in_specs=[
            spec,
            pl.BlockSpec(block, lambda i: (jnp.minimum(i, 1), 0, 0)),
            pl.BlockSpec(block, lambda i: (jnp.maximum(i - 2, 0), 0, 0)),
        ],
        out_specs=spec,
        out_shape=pltpu.HBM(own.shape, BF16),
        compiler_params=pltpu.CompilerParams(vmem_limit_bytes=16 << 20),
        cost_estimate=SMALL,
        name="add_parts",
    )(own, low, high)


def combine_kernel(x_ref, main_ref, last_ref, gate_ref, sum_ref, o_ref, rows):
    whole = CHIPS * 8
    extra = rows.shape[0] > whole
    unpack(x_ref, rows, extra)
    at = lax.broadcasted_iota(jnp.int32, (2 * ROWS, rows.shape[0]), 1)
    code = (at >> 4) * 8 + (at & 7)
    if extra:
        in_last = at >= whole
        code = jnp.where(in_last, ((at - whole) >> 2) * 2 + (at & 1), code + 256)
        wanted = jnp.where(in_last, last_ref[...], main_ref[...])
    else:
        wanted = main_ref[...]
    picked = dot((code == wanted).astype(F32).astype(BF16), rows[...])
    mix = picked[0:ROWS] * gate_ref[:, 0:1] + picked[ROWS:] * gate_ref[:, 1:2]
    o_ref[...] = (sum_ref[...] + mix).astype(o_ref.dtype)


def combine(returned, main, last, gates, total, dtype):
    count = CHIPS * (8 if returned.shape[1] == PACKS[0] else 10)
    return pl.pallas_call(
        combine_kernel,
        out_shape=pltpu.HBM((ROWS, D), dtype),
        scratch_shapes=[pltpu.VMEM((count, D), BF16)],
        compiler_params=pltpu.CompilerParams(vmem_limit_bytes=VMEM),
        cost_estimate=pl.CostEstimate(
            flops=4 * ROWS * count * D, bytes_accessed=2 * returned.size, transcendentals=0
        ),
        name="combine",
    )(in_hbm(returned), main, last, gates, in_hbm(total))


def shards(
    patches,
    temporal_q,
    temporal_k,
    temporal_v,
    clip_lengths,
    w_time,
    gain_space,
    w_space,
    w_merge,
    gain_mix,
    expert_ids,
    gate_weights,
    w_expand,
    w_reduce,
):
    frame_axes, chip_axes = ("x", "y"), ("x", "y", "z")
    swap = [(0, 1), (1, 0)]

    own_rows = lax.dynamic_slice(
        w_space,
        (lax.axis_index("z") * 384, lax.axis_index("c") * 144),
        (384, 144),
    ).T
    w_rows = lax.all_gather(own_rows, ("x", "y", "z", "c"), axis=0, tiled=True)
    w_rows = w_rows.reshape(FRAMES, 4, 288, 384)

    qkv_own = jnp.concatenate(
        [a.reshape(FRAMES, 16, D) for a in (temporal_q, temporal_k, temporal_v)], axis=1
    )
    qkv = lax.all_to_all(qkv_own, frame_axes, split_axis=0, concat_axis=0, tiled=True)
    mixed = time_attention(clip_lengths, qkv)
    mixed = lax.all_to_all(mixed, frame_axes, split_axis=0, concat_axis=0, tiled=True)
    after_time, normed = after_time_step(
        mixed.reshape(ROWS, D), patches.reshape(ROWS, D), w_time, gain_space.reshape(1, D)
    )

    experts = expert_ids.reshape(ROWS * 2)
    index = jnp.arange(ROWS * 2, dtype=jnp.int32)
    earlier = (experts[:, None] == experts[None, :]) & (index[None, :] < index[:, None])
    slot = jnp.sum(earlier.astype(jnp.int32), axis=1)
    main = jnp.where(slot < MAIN, (slot // 8) * 256 + experts * 8 + slot % 8, -1).reshape(ROWS, 2)
    last = jnp.where(slot >= MAIN, experts * 2 + slot - MAIN, -1).reshape(ROWS, 2)

    after_space, *outgoing = space_step(
        normed, w_rows, w_merge, after_time, gain_mix.reshape(1, D), main.T, last.T
    )

    def exchange(chunks):
        return lax.all_to_all(chunks, chip_axes, split_axis=0, concat_axis=0, tiled=True)

    def expert_sums(arrived):
        theirs = lax.ppermute(arrived, "c", swap)
        own, low, high = run_experts(arrived, theirs, w_expand, w_reduce)
        return add_parts(own, lax.ppermute(low, "c", swap), lax.ppermute(high, "c", swap))

    arrived_a, arrived_b = (exchange(o.reshape(CHIPS, -1, 128)) for o in outgoing)
    arrived_b, sums_a = lax.optimization_barrier((arrived_b, expert_sums(arrived_a)))
    returned_a = exchange(sums_a)
    returned_a, sums_b = lax.optimization_barrier((returned_a, expert_sums(arrived_b)))
    returned_b = exchange(sums_b)
    main, last = (codes.T.reshape(2 * ROWS, 1) for codes in (main, last))
    gates = gate_weights.reshape(ROWS, 2)
    total = combine(returned_a, main, last, gates, after_space, F32)
    out = combine(returned_b, main, last, gates, total, BF16)
    return out.reshape(patches.shape)


def solution(mesh):
    grid = Mesh(mesh.devices.reshape(4, 4, 4, 2), ("x", "y", "z", "c"))
    frame, clip = ("x", "y"), ("z", "c")
    every = ("x", "y", "z", "c")
    return jax.shard_map(
        shards,
        mesh=grid,
        in_specs=(
            P(frame, clip, None, None),
            P(frame, clip, None, None),
            P(frame, clip, None, None),
            P(frame, clip, None, None),
            P(clip),
            P(),
            P(),
            P(None, frame),
            P(),
            P(),
            P(frame, clip, None, None),
            P(frame, clip, None, None),
            P(every, None, None),
            P(every, None, None),
        ),
        out_specs=P(frame, clip, None, None),
        check_vma=False,
    )
```

```python
import math
from functools import partial

import jax
import jax.numpy as jnp
from jax import lax
from jax.experimental import pallas as pl
from jax.experimental.pallas import tpu as pltpu
from jax.sharding import Mesh, PartitionSpec as P

HEADS = 24
HEAD = 64
EXPERTS = 32
D = 1536
ROWS = 256
FRAMES = 16
MAIN = 16
PACK = 224
BLOCKS = D // 128
EPSILON = 1e-06
F32 = jnp.float32
BF16 = jnp.bfloat16
VMEM = 40 << 20


def dot(a, b):
    return jnp.dot(a, b, preferred_element_type=F32)


def dot_nt(a, b):
    return lax.dot_general(a, b, (((1,), (1,)), ((), ())), preferred_element_type=F32)


def in_vmem(array):
    return pltpu.with_memory_space_constraint(array, pltpu.VMEM)


def in_hbm(array):
    return pltpu.with_memory_space_constraint(array, pltpu.HBM)


def attend_pair(q, k, v, keep=None):
    low = lax.broadcasted_iota(jnp.int32, (ROWS, 128), 1) < HEAD
    zero, one = jnp.zeros((ROWS, 128), BF16), jnp.ones((ROWS, 128), BF16)
    parts = []
    for mine in (low, ~low):
        scores = dot_nt(q, jnp.where(mine, k, zero))
        if keep is not None:
            scores = jnp.where(keep, scores, -1e30)
        top = jnp.max(scores, axis=-1, keepdims=True)
        powers = jnp.exp2((scores - top) * (1.0 / (math.sqrt(HEAD) * math.log(2.0))))
        parts.append(dot(powers.astype(BF16), jnp.where(mine, v, one)))
    sums = pltpu.roll(jnp.where(low, parts[1], parts[0]), HEAD, 1)
    return (jnp.where(low, parts[0], parts[1]) / sums).astype(BF16)


def norm_rows(values, gain):
    centre = values - jnp.mean(values, axis=-1, keepdims=True)
    spread = jnp.mean(centre * centre, axis=-1, keepdims=True)
    return (centre * lax.rsqrt(spread + EPSILON) * gain).astype(BF16)


TIME_PAIRS = 3


def time_kernel(len_ref, x_ref, o_ref):
    row = lax.broadcasted_iota(jnp.int32, (ROWS, ROWS), 0)
    col = lax.broadcasted_iota(jnp.int32, (ROWS, ROWS), 1)
    keep = ((row & 15) == (col & 15)) & ((col >> 4) < len_ref[0])

    def heads(step, carry):
        for pair in range(TIME_PAIRS):
            lanes = pl.ds(pl.multiple_of((step * TIME_PAIRS + pair) * 128, 128), 128)
            q = x_ref[:, 0:16, lanes].reshape(ROWS, 128)
            k = x_ref[:, 16:32, lanes].reshape(ROWS, 128)
            v = x_ref[:, 32:48, lanes].reshape(ROWS, 128)
            o_ref[:, :, lanes] = attend_pair(q, k, v, keep).reshape(FRAMES, 16, 128)
        return carry

    lax.fori_loop(0, BLOCKS // TIME_PAIRS, heads, 0)


def time_attention(lengths, qkv):
    return pl.pallas_call(
        time_kernel,
        in_specs=[
            pl.BlockSpec(memory_space=pltpu.SMEM),
            pl.BlockSpec(memory_space=pltpu.VMEM),
        ],
        out_shape=jax.ShapeDtypeStruct((FRAMES, 16, D), BF16),
        compiler_params=pltpu.CompilerParams(vmem_limit_bytes=16 << 20),
        name="time_attention",
    )(lengths, in_vmem(qkv))


def after_time_kernel(mixed_ref, patch_ref, w_ref, gain_ref, after_ref, normed_ref):
    after_time = patch_ref[...].astype(F32) + dot(mixed_ref[...], w_ref[...])
    after_ref[...] = after_time
    normed_ref[...] = norm_rows(after_time, gain_ref[...])


def after_time_step(mixed, patches, w_time, gain):
    return pl.pallas_call(
        after_time_kernel,
        out_shape=[
            jax.ShapeDtypeStruct((ROWS, D), F32),
            jax.ShapeDtypeStruct((ROWS, D), BF16),
        ],
        compiler_params=pltpu.CompilerParams(vmem_limit_bytes=24 << 20),
        name="after_time",
    )(mixed, patches, in_hbm(w_time), gain)


def spread_matrix():
    i = lax.broadcasted_iota(jnp.int32, (256, 192), 0)
    j = lax.broadcasted_iota(jnp.int32, (256, 192), 1)
    same = (i >> 5) == ((j & 15) >> 1)
    place = (i & 31) == 2 * (j >> 4) + (j & 1)
    return (same & place).astype(F32).astype(BF16)


def gather_matrix():
    j = lax.broadcasted_iota(jnp.int32, (192, 256), 0)
    i = lax.broadcasted_iota(jnp.int32, (192, 256), 1)
    same = (i >> 5) == ((j & 15) >> 1)
    place = (i & 31) == 2 * (j >> 4) + (j & 1)
    return (same & place).astype(F32).astype(BF16)


def unpack(block_ref, rows_ref, chunks):
    pick = gather_matrix()
    whole = chunks * 16
    for j in range(BLOCKS):
        rows_ref[0:whole, j * 128 : (j + 1) * 128] = block_ref[
            :, j * 16 : (j + 1) * 16, :
        ].reshape(whole, 128)
    for group in range(chunks // 8):
        packed = block_ref[group * 8 : (group + 1) * 8, 192:224, :].reshape(256, 128)
        last = dot(pick, packed).astype(BF16)
        at = whole + group * 16
        for j in range(BLOCKS):
            rows_ref[at : at + 16, j * 128 : (j + 1) * 128] = last[j * 16 : (j + 1) * 16, :]


GROUPS = ((0, 1, 5, 6, 10, 11), (2, 7, 12, 13), (3, 8, 9, 14), (4, 15))
QUARTER = D // len(GROUPS)


def space_kernel(
    normed_ref,
    w_hbm,
    merge_hbm,
    after_ref,
    gain_ref,
    main_ref,
    last_ref,
    space_ref,
    send_ref,
    w_rows,
    merge,
    spatial,
    sems,
):
    def fetch(group, frame, z):
        return pltpu.make_async_copy(
            w_hbm.at[frame, z],
            w_rows.at[pl.ds(frame * 288, 288), pl.ds(z * 384, 384)],
            sems.at[group],
        )

    pieces = [[(frame, z) for frame in frames for z in range(4)] for frames in GROUPS]
    for group in range(len(GROUPS)):
        for count, (frame, z) in enumerate(pieces[group]):
            fetch(group, frame, z).start(priority=count % 2)
    fetch_merge = pltpu.make_async_copy(merge_hbm, merge, sems.at[len(GROUPS)])
    fetch_merge.start()
    for group in range(len(GROUPS)):
        for frame, z in pieces[group]:
            fetch(group, frame, z).wait()
        q_all, k_all, v_all = (
            dot_nt(
                normed_ref[...], w_rows[part * D + group * QUARTER : part * D + (group + 1) * QUARTER]
            ).astype(BF16)
            for part in range(3)
        )
        for pair in range(QUARTER // 128):
            lanes = slice(pair * 128, (pair + 1) * 128)
            q, k, v = q_all[:, lanes], k_all[:, lanes], v_all[:, lanes]
            at = group * QUARTER + pair * 128
            spatial[:, at : at + 128] = attend_pair(q, k, v)
    fetch_merge.wait()
    after_space = after_ref[...] + dot(spatial[...], merge[...])
    space_ref[...] = after_space
    mixed_in = norm_rows(after_space, gain_ref[...])
    slot = lax.broadcasted_iota(jnp.int32, (512, ROWS), 0)
    chosen = (slot == main_ref[0:1, :]) | (slot == main_ref[1:2, :])
    rows = dot(chosen.astype(F32).astype(BF16), mixed_in).astype(BF16)
    slot = lax.broadcasted_iota(jnp.int32, (64, ROWS), 0)
    chosen = (slot == last_ref[0:1, :]) | (slot == last_ref[1:2, :])
    last = dot(chosen.astype(F32).astype(BF16), mixed_in).astype(BF16)
    for j in range(BLOCKS):
        piece = rows[:, j * 128 : (j + 1) * 128].reshape(EXPERTS, 16, 128)
        for copy in range(2):
            send_ref[:, copy, j * 16 : (j + 1) * 16, :] = piece
    spread = spread_matrix()
    for group in range(4):
        own = last[group * 16 : (group + 1) * 16, :]
        tall = jnp.concatenate([own[:, j * 128 : (j + 1) * 128] for j in range(BLOCKS)], axis=0)
        packed = dot(spread, tall).astype(BF16).reshape(8, 32, 128)
        for copy in range(2):
            send_ref[group * 8 : (group + 1) * 8, copy, 192:224, :] = packed


def space_step(normed, w_rows, w_merge, after_time, gain, main, last):
    resident = pl.BlockSpec(memory_space=pltpu.VMEM)
    anywhere = pl.BlockSpec(memory_space=pl.ANY)
    return pl.pallas_call(
        space_kernel,
        in_specs=[resident, anywhere, anywhere] + [resident] * 4,
        out_specs=[resident] * 2,
        out_shape=[
            pltpu.VMEM((ROWS, D), F32),
            pltpu.VMEM((EXPERTS, 2, PACK, 128), BF16),
        ],
        scratch_shapes=[
            pltpu.VMEM((3 * D, D), BF16),
            pltpu.VMEM((D, D), BF16),
            pltpu.VMEM((ROWS, D), BF16),
            pltpu.SemaphoreType.DMA((len(GROUPS) + 1,)),
        ],
        compiler_params=pltpu.CompilerParams(vmem_limit_bytes=32 << 20),
        name="space_attention",
    )(
        in_vmem(normed),
        in_hbm(w_rows),
        in_hbm(w_merge),
        *(in_vmem(a) for a in (after_time, gain, main, last)),
    )


CHUNKS = 32
EXPERT_ROWS = CHUNKS * 18
CUT = 512
CUTS = D // CUT


def first_kernel(half, x_ref, expand_hbm, reduce_hbm, o_ref, expand, reduce, rows, hidden, sems):
    def fetch(n):
        cols = pl.ds((n % CUTS) * CUT, CUT)
        source, target = (expand_hbm, expand) if n < CUTS else (reduce_hbm, reduce)
        return pltpu.make_async_copy(source.at[:, :, cols], target.at[:, :, cols], sems.at[n])

    for n in range(2 * CUTS):
        fetch(n).start()
    expert_body(half, x_ref, expand, reduce, o_ref, rows, hidden, lambda n: fetch(n).wait())


def later_kernel(half, x_ref, expand, reduce, o_ref, rows, hidden):
    expert_body(half, x_ref, expand, reduce, o_ref, rows, hidden, lambda n: None)


def add_kernel(own_a, back_a, own_b, back_b, o_ref):
    step = pl.program_id(0)

    @pl.when(step < 2)
    def _():
        o_ref[...] = (own_a[...].astype(F32) + back_a[...].astype(F32)).astype(BF16)

    @pl.when(step >= 2)
    def _():
        o_ref[...] = (own_b[...].astype(F32) + back_b[...].astype(F32)).astype(BF16)


def add_parts(own_a, back_a, own_b, back_b):
    block = (CHUNKS // 2, PACK, 128)
    first = pl.BlockSpec(block, lambda i: (jnp.minimum(i, 1), 0, 0))
    second = pl.BlockSpec(block, lambda i: (jnp.maximum(i - 2, 0), 0, 0))
    return pl.pallas_call(
        add_kernel,
        grid=(4,),
        in_specs=[first, first, second, second],
        out_specs=pl.BlockSpec(block, lambda i: (i, 0, 0)),
        out_shape=pltpu.HBM((2 * CHUNKS, PACK, 128), BF16),
        compiler_params=pltpu.CompilerParams(vmem_limit_bytes=16 << 20),
        name="add_parts",
    )(own_a, back_a, own_b, back_b)


def expert_body(half, x_ref, expand, reduce, o_ref, rows, hidden, ready):
    whole = CHUNKS * 16
    unpack(x_ref.at[half * CHUNKS : (half + 1) * CHUNKS], rows, CHUNKS)
    for n in range(CUTS):
        ready(n)
        inner = dot(rows[...], expand[0, :, n * CUT : (n + 1) * CUT])
        active = inner * (0.5 + 0.5 * lax.erf(inner * math.sqrt(0.5)))
        hidden[:, n * CUT : (n + 1) * CUT] = active.astype(BF16)
    spread = spread_matrix()
    tops = [[] for _ in range(CHUNKS // 8)]
    for n in range(CUTS):
        ready(CUTS + n)
        part = dot(hidden[...], reduce[0, :, n * CUT : (n + 1) * CUT])
        for j in range(CUT // 128):
            at = n * (CUT // 128) + j
            piece = part[:, j * 128 : (j + 1) * 128]
            main = piece[0:whole].reshape(CHUNKS, 16, 128)
            o_ref[:, at * 16 : (at + 1) * 16, :] = main.astype(BF16)
            for group in range(CHUNKS // 8):
                start = whole + group * 16
                tops[group].append(piece[start : start + 16].astype(BF16))
    for group in range(CHUNKS // 8):
        packed = dot(spread, jnp.concatenate(tops[group], axis=0)).reshape(8, 32, 128)
        at = group * 8
        o_ref[at : at + 8, 192:224, :] = packed.astype(BF16)


EXPERT_SCRATCH = [
    pltpu.VMEM((EXPERT_ROWS, D), BF16),
    pltpu.VMEM((EXPERT_ROWS, D), BF16),
]
EXPERT_COST = pl.CostEstimate(
    flops=EXPERT_ROWS * D * D * 4,
    bytes_accessed=2 * CHUNKS * PACK * 128 * 2,
    transcendentals=EXPERT_ROWS * D,
)
HALF = (CHUNKS, PACK, 128)


RESIDENT = pl.BlockSpec(memory_space=pltpu.VMEM)


def first_experts(arrived, expand, reduce):
    anywhere = pl.BlockSpec(memory_space=pl.ANY)
    return pl.pallas_call(
        partial(first_kernel, 0),
        in_specs=[RESIDENT, anywhere, anywhere],
        out_specs=[RESIDENT] * 3,
        out_shape=[
            pltpu.VMEM(HALF, BF16),
            pltpu.VMEM((1, D, D), BF16),
            pltpu.VMEM((1, D, D), BF16),
        ],
        scratch_shapes=EXPERT_SCRATCH + [pltpu.SemaphoreType.DMA((2 * CUTS,))],
        compiler_params=pltpu.CompilerParams(vmem_limit_bytes=16 << 20),
        cost_estimate=EXPERT_COST,
        name="experts",
    )(in_vmem(arrived), in_hbm(expand), in_hbm(reduce))


def run_experts(half, arrived, expand, reduce):
    return pl.pallas_call(
        partial(later_kernel, half),
        in_specs=[RESIDENT] * 3,
        out_specs=RESIDENT,
        out_shape=pltpu.VMEM(HALF, BF16),
        scratch_shapes=EXPERT_SCRATCH,
        compiler_params=pltpu.CompilerParams(vmem_limit_bytes=16 << 20),
        cost_estimate=EXPERT_COST,
        name="experts",
    )(in_vmem(arrived), in_vmem(expand), in_vmem(reduce))


def combine_kernel(x_hbm, main_ref, last_ref, gate_ref, space_ref, o_ref, chunks, rows, sems):
    def fetch(part):
        at = pl.ds(part * CHUNKS, CHUNKS)
        return pltpu.make_async_copy(x_hbm.at[at], chunks.at[at], sems.at[part])

    for part in range(2):
        fetch(part).start()
    at = lax.broadcasted_iota(jnp.int32, (2 * ROWS, EXPERT_ROWS), 1)
    in_last = at >= CHUNKS * MAIN
    last_code = ((at - CHUNKS * MAIN) >> 2) * 2 + (at & 1)
    main_code = (at >> 5) * MAIN + (at & 15)
    code = jnp.where(in_last, last_code, main_code)
    wanted = jnp.where(in_last, last_ref[...], main_ref[...])
    step = jnp.where(in_last, CHUNKS, CHUNKS // 2 * MAIN)
    picked = None
    for part in range(2):
        fetch(part).wait()
        half = rows.at[part * EXPERT_ROWS : (part + 1) * EXPERT_ROWS]
        unpack(chunks.at[part * CHUNKS : (part + 1) * CHUNKS], half, CHUNKS)
        chosen = (code + part * step == wanted).astype(F32).astype(BF16)
        term = dot(chosen, half[...])
        picked = term if picked is None else picked + term
    mix = picked[0:ROWS] * gate_ref[:, 0:1] + picked[ROWS:] * gate_ref[:, 1:2]
    o_ref[...] = (space_ref[...] + mix).astype(BF16)


def combine(returned, main, last, gates, after_space):
    return pl.pallas_call(
        combine_kernel,
        in_specs=[pl.BlockSpec(memory_space=pl.ANY)] + [pl.BlockSpec(memory_space=pltpu.VMEM)] * 4,
        out_shape=jax.ShapeDtypeStruct((ROWS, D), BF16),
        scratch_shapes=[
            pltpu.VMEM((2 * CHUNKS, PACK, 128), BF16),
            pltpu.VMEM((2 * EXPERT_ROWS, D), BF16),
            pltpu.SemaphoreType.DMA((2,)),
        ],
        compiler_params=pltpu.CompilerParams(vmem_limit_bytes=VMEM),
        name="combine",
    )(in_hbm(returned), *map(in_vmem, (main, last, gates, after_space)))


def shards(
    patches,
    temporal_q,
    temporal_k,
    temporal_v,
    clip_lengths,
    w_time,
    gain_space,
    w_space,
    w_merge,
    gain_mix,
    expert_ids,
    gate_weights,
    w_expand,
    w_reduce,
):
    frame_axes, chip_axes = ("x", "y"), ("x", "y", "z")
    swap = [(0, 1), (1, 0)]

    own_rows = lax.dynamic_slice(
        w_space,
        (lax.axis_index("z") * 384, lax.axis_index("c") * 144),
        (384, 144),
    ).T
    w_rows = lax.all_gather(own_rows, ("x", "y", "z", "c"), axis=0, tiled=True)
    w_rows = w_rows.reshape(FRAMES, 4, 288, 384)

    qkv_own = jnp.concatenate(
        [a.reshape(FRAMES, 16, D) for a in (temporal_q, temporal_k, temporal_v)], axis=1
    )
    qkv = lax.all_to_all(qkv_own, frame_axes, split_axis=0, concat_axis=0, tiled=True)
    mixed = time_attention(clip_lengths, qkv)
    mixed = lax.all_to_all(mixed, frame_axes, split_axis=0, concat_axis=0, tiled=True)
    after_time, normed = after_time_step(
        mixed.reshape(ROWS, D), patches.reshape(ROWS, D), w_time, gain_space.reshape(1, D)
    )

    experts = expert_ids.reshape(ROWS * 2)
    index = jnp.arange(ROWS * 2, dtype=jnp.int32)
    earlier = (experts[:, None] == experts[None, :]) & (index[None, :] < index[:, None])
    slot = jnp.sum(earlier.astype(jnp.int32), axis=1)
    main = jnp.where(slot < MAIN, experts * MAIN + slot, -1).reshape(ROWS, 2)
    last = jnp.where(slot >= MAIN, experts * 2 + slot - MAIN, -1).reshape(ROWS, 2)

    after_space, outgoing = space_step(
        normed, w_rows, w_merge, after_time, gain_mix.reshape(1, D), main.T, last.T
    )
    arrived = lax.all_to_all(
        outgoing.reshape(64, PACK, 128), chip_axes, split_axis=0, concat_axis=0, tiled=True
    )
    theirs = lax.ppermute(arrived, "c", swap)
    part_own, expand, reduce = first_experts(arrived, w_expand, w_reduce)
    theirs, part_own = lax.optimization_barrier((theirs, part_own))
    part_a = run_experts(0, theirs, expand, reduce)
    back_a = lax.ppermute(part_a, "c", swap)
    part_b = run_experts(1, theirs, expand, reduce)
    back_b = lax.ppermute(part_b, "c", swap)
    part_own_b = run_experts(1, arrived, expand, reduce)
    sums = add_parts(part_own, back_a, part_own_b, back_b)
    returned = lax.all_to_all(sums, chip_axes, split_axis=0, concat_axis=0, tiled=True)
    main, last = (codes.T.reshape(2 * ROWS, 1) for codes in (main, last))
    out = combine(returned, main, last, gate_weights.reshape(ROWS, 2), after_space)
    return out.reshape(patches.shape)


def solution(mesh):
    grid = Mesh(mesh.devices.reshape(4, 4, 4, 2), ("x", "y", "z", "c"))
    frame, clip = ("x", "y"), ("z", "c")
    every = ("x", "y", "z", "c")
    return jax.shard_map(
        shards,
        mesh=grid,
        in_specs=(
            P(frame, clip, None, None),
            P(frame, clip, None, None),
            P(frame, clip, None, None),
            P(frame, clip, None, None),
            P(clip),
            P(),
            P(),
            P(None, frame),
            P(),
            P(),
            P(frame, clip, None, None),
            P(frame, clip, None, None),
            P(every, None, None),
            P(every, None, None),
        ),
        out_specs=P(frame, clip, None, None),
        check_vma=False,
    )
```

```python
import math
from functools import partial

import jax
import jax.numpy as jnp
from jax import lax
from jax.experimental import pallas as pl
from jax.experimental.pallas import tpu as pltpu
from jax.sharding import Mesh, PartitionSpec as P

HEADS = 24
HEAD = 64
EXPERTS = 32
D = 1536
ROWS = 256
FRAMES = 16
MAIN = 16
PACK = 224
BLOCKS = D // 128
EPSILON = 1e-06
F32 = jnp.float32
BF16 = jnp.bfloat16
VMEM = 40 << 20


def dot(a, b):
    return jnp.dot(a, b, preferred_element_type=F32)


def dot_nt(a, b):
    return lax.dot_general(a, b, (((1,), (1,)), ((), ())), preferred_element_type=F32)


def in_vmem(array):
    return pltpu.with_memory_space_constraint(array, pltpu.VMEM)


def in_hbm(array):
    return pltpu.with_memory_space_constraint(array, pltpu.HBM)


def attend_pair(q, k, v, keep=None):
    low = lax.broadcasted_iota(jnp.int32, (ROWS, 128), 1) < HEAD
    zero, one = jnp.zeros((ROWS, 128), BF16), jnp.ones((ROWS, 128), BF16)
    parts = []
    for mine in (low, ~low):
        scores = dot_nt(q, jnp.where(mine, k, zero))
        if keep is not None:
            scores = jnp.where(keep, scores, -1e30)
        top = jnp.max(scores, axis=-1, keepdims=True)
        powers = jnp.exp2((scores - top) * (1.0 / (math.sqrt(HEAD) * math.log(2.0))))
        parts.append(dot(powers.astype(BF16), jnp.where(mine, v, one)))
    sums = pltpu.roll(jnp.where(low, parts[1], parts[0]), HEAD, 1)
    return (jnp.where(low, parts[0], parts[1]) / sums).astype(BF16)


def norm_rows(values, gain):
    centre = values - jnp.mean(values, axis=-1, keepdims=True)
    spread = jnp.mean(centre * centre, axis=-1, keepdims=True)
    return (centre * lax.rsqrt(spread + EPSILON) * gain).astype(BF16)


TIME_PAIRS = 3


def time_kernel(len_ref, x_ref, o_ref):
    row = lax.broadcasted_iota(jnp.int32, (ROWS, ROWS), 0)
    col = lax.broadcasted_iota(jnp.int32, (ROWS, ROWS), 1)
    keep = ((row & 15) == (col & 15)) & ((col >> 4) < len_ref[0])

    def heads(step, carry):
        for pair in range(TIME_PAIRS):
            lanes = pl.ds(pl.multiple_of((step * TIME_PAIRS + pair) * 128, 128), 128)
            q = x_ref[:, 0:16, lanes].reshape(ROWS, 128)
            k = x_ref[:, 16:32, lanes].reshape(ROWS, 128)
            v = x_ref[:, 32:48, lanes].reshape(ROWS, 128)
            o_ref[:, :, lanes] = attend_pair(q, k, v, keep).reshape(FRAMES, 16, 128)
        return carry

    lax.fori_loop(0, BLOCKS // TIME_PAIRS, heads, 0)


def time_attention(lengths, qkv):
    return pl.pallas_call(
        time_kernel,
        in_specs=[
            pl.BlockSpec(memory_space=pltpu.SMEM),
            pl.BlockSpec(memory_space=pltpu.VMEM),
        ],
        out_shape=jax.ShapeDtypeStruct((FRAMES, 16, D), BF16),
        compiler_params=pltpu.CompilerParams(vmem_limit_bytes=16 << 20),
        name="time_attention",
    )(lengths, in_vmem(qkv))


def after_time_kernel(mixed_ref, patch_ref, w_ref, gain_ref, after_ref, normed_ref):
    after_time = patch_ref[...].astype(F32) + dot(mixed_ref[...], w_ref[...])
    after_ref[...] = after_time
    normed_ref[...] = norm_rows(after_time, gain_ref[...])


def after_time_step(mixed, patches, w_time, gain):
    return pl.pallas_call(
        after_time_kernel,
        out_shape=[
            jax.ShapeDtypeStruct((ROWS, D), F32),
            jax.ShapeDtypeStruct((ROWS, D), BF16),
        ],
        compiler_params=pltpu.CompilerParams(vmem_limit_bytes=24 << 20),
        name="after_time",
    )(mixed, patches, in_hbm(w_time), gain)


def spread_matrix():
    i = lax.broadcasted_iota(jnp.int32, (256, 192), 0)
    j = lax.broadcasted_iota(jnp.int32, (256, 192), 1)
    same = (i >> 5) == ((j & 15) >> 1)
    place = (i & 31) == 2 * (j >> 4) + (j & 1)
    return (same & place).astype(F32).astype(BF16)


def gather_matrix():
    j = lax.broadcasted_iota(jnp.int32, (192, 256), 0)
    i = lax.broadcasted_iota(jnp.int32, (192, 256), 1)
    same = (i >> 5) == ((j & 15) >> 1)
    place = (i & 31) == 2 * (j >> 4) + (j & 1)
    return (same & place).astype(F32).astype(BF16)


def unpack(block_ref, rows_ref, chunks):
    pick = gather_matrix()
    whole = chunks * 16
    for j in range(BLOCKS):
        rows_ref[0:whole, j * 128 : (j + 1) * 128] = block_ref[
            :, j * 16 : (j + 1) * 16, :
        ].reshape(whole, 128)
    for group in range(chunks // 8):
        packed = block_ref[group * 8 : (group + 1) * 8, 192:224, :].reshape(256, 128)
        last = dot(pick, packed).astype(BF16)
        at = whole + group * 16
        for j in range(BLOCKS):
            rows_ref[at : at + 16, j * 128 : (j + 1) * 128] = last[j * 16 : (j + 1) * 16, :]


GROUPS = 4
PAIRS = 4


def space_kernel(
    normed_ref,
    w_hbm,
    merge_hbm,
    after_ref,
    gain_ref,
    main_ref,
    last_ref,
    space_ref,
    send_ref,
    w_rows,
    merge,
    projected,
    spatial,
    total,
    sems,
):
    per_group = FRAMES // GROUPS
    wide = per_group * 288

    def fetch(group, frame, z):
        f = group * per_group + frame
        return pltpu.make_async_copy(
            w_hbm.at[f, z],
            w_rows.at[pl.ds(f * 288, 288), pl.ds(z * 384, 384)],
            sems.at[group],
        )

    pieces = [(frame, z) for frame in range(per_group) for z in range(4)]
    for group in range(GROUPS):
        for frame, z in pieces:
            fetch(group, frame, z).start()
    fetch_merge = pltpu.make_async_copy(merge_hbm, merge, sems.at[GROUPS])
    fetch_merge.start()
    for group in range(GROUPS):
        for frame, z in pieces:
            fetch(group, frame, z).wait()
        rows = slice(group * wide, (group + 1) * wide)
        projected[:, rows] = dot_nt(normed_ref[...], w_rows[rows, :]).astype(BF16)

    def heads(step, carry):
        for pair in range(PAIRS):
            first = pl.multiple_of((step * PAIRS + pair) * 128, 128)
            q, k, v = (
                projected[:, pl.ds(pl.multiple_of(first + part * D, 128), 128)] for part in range(3)
            )
            spatial[:, pl.ds(first, 128)] = attend_pair(q, k, v)
        return carry

    lax.fori_loop(0, BLOCKS // PAIRS, heads, 0)
    fetch_merge.wait()
    after_space = after_ref[...] + dot(spatial[...], merge[...])
    total[...] = after_space
    keep = pltpu.make_async_copy(total, space_ref, sems.at[GROUPS + 1])
    keep.start()
    mixed_in = norm_rows(after_space, gain_ref[...])
    slot = lax.broadcasted_iota(jnp.int32, (512, ROWS), 0)
    chosen = (slot == main_ref[0:1, :]) | (slot == main_ref[1:2, :])
    rows = dot(chosen.astype(F32).astype(BF16), mixed_in).astype(BF16)
    slot = lax.broadcasted_iota(jnp.int32, (64, ROWS), 0)
    chosen = (slot == last_ref[0:1, :]) | (slot == last_ref[1:2, :])
    last = dot(chosen.astype(F32).astype(BF16), mixed_in).astype(BF16)
    for j in range(BLOCKS):
        piece = rows[:, j * 128 : (j + 1) * 128].reshape(EXPERTS, 16, 128)
        for copy in range(2):
            send_ref[:, copy, j * 16 : (j + 1) * 16, :] = piece
    spread = spread_matrix()
    for group in range(4):
        own = last[group * 16 : (group + 1) * 16, :]
        tall = jnp.concatenate([own[:, j * 128 : (j + 1) * 128] for j in range(BLOCKS)], axis=0)
        packed = dot(spread, tall).astype(BF16).reshape(8, 32, 128)
        for copy in range(2):
            send_ref[group * 8 : (group + 1) * 8, copy, 192:224, :] = packed
    keep.wait()


def space_step(normed, w_rows, w_merge, after_time, gain, main, last):
    resident = pl.BlockSpec(memory_space=pltpu.VMEM)
    anywhere = pl.BlockSpec(memory_space=pl.ANY)
    return pl.pallas_call(
        space_kernel,
        in_specs=[resident, anywhere, anywhere] + [resident] * 4,
        out_specs=[anywhere, resident],
        out_shape=[
            pltpu.HBM((ROWS, D), F32),
            pltpu.VMEM((EXPERTS, 2, PACK, 128), BF16),
        ],
        scratch_shapes=[
            pltpu.VMEM((3 * D, D), BF16),
            pltpu.VMEM((D, D), BF16),
            pltpu.VMEM((ROWS, 3 * D), BF16),
            pltpu.VMEM((ROWS, D), BF16),
            pltpu.VMEM((ROWS, D), F32),
            pltpu.SemaphoreType.DMA((GROUPS + 2,)),
        ],
        compiler_params=pltpu.CompilerParams(vmem_limit_bytes=32 << 20),
        name="space_attention",
    )(
        in_vmem(normed),
        in_hbm(w_rows),
        in_hbm(w_merge),
        *(in_vmem(a) for a in (after_time, gain, main, last)),
    )


CHUNKS = 32
EXPERT_ROWS = CHUNKS * 18
CUT = 512
CUTS = D // CUT


def later_kernel(half, x_ref, expand, reduce, o_ref, rows, hidden):
    expert_body(half, x_ref, expand, reduce, o_ref, rows, hidden, lambda n: None)


def add_kernel(own_a, back_a, own_b, back_b, o_ref):
    step = pl.program_id(0)

    @pl.when(step < 2)
    def _():
        o_ref[...] = (own_a[...].astype(F32) + back_a[...].astype(F32)).astype(BF16)

    @pl.when(step >= 2)
    def _():
        o_ref[...] = (own_b[...].astype(F32) + back_b[...].astype(F32)).astype(BF16)


def add_parts(own_a, back_a, own_b, back_b):
    block = (CHUNKS // 2, PACK, 128)
    first = pl.BlockSpec(block, lambda i: (jnp.minimum(i, 1), 0, 0))
    second = pl.BlockSpec(block, lambda i: (jnp.maximum(i - 2, 0), 0, 0))
    return pl.pallas_call(
        add_kernel,
        grid=(4,),
        in_specs=[first, first, second, second],
        out_specs=pl.BlockSpec(block, lambda i: (i, 0, 0)),
        out_shape=pltpu.HBM((2 * CHUNKS, PACK, 128), BF16),
        compiler_params=pltpu.CompilerParams(vmem_limit_bytes=16 << 20),
        name="add_parts",
    )(own_a, back_a, own_b, back_b)


def expert_body(half, x_ref, expand, reduce, o_ref, rows, hidden, ready):
    whole = CHUNKS * 16
    unpack(x_ref.at[half * CHUNKS : (half + 1) * CHUNKS], rows, CHUNKS)
    for n in range(CUTS):
        ready(n)
        inner = dot(rows[...], expand[0, :, n * CUT : (n + 1) * CUT])
        active = inner * (0.5 + 0.5 * lax.erf(inner * math.sqrt(0.5)))
        hidden[:, n * CUT : (n + 1) * CUT] = active.astype(BF16)
    spread = spread_matrix()
    tops = [[] for _ in range(CHUNKS // 8)]
    for n in range(CUTS):
        ready(CUTS + n)
        part = dot(hidden[...], reduce[0, :, n * CUT : (n + 1) * CUT])
        for j in range(CUT // 128):
            at = n * (CUT // 128) + j
            piece = part[:, j * 128 : (j + 1) * 128]
            main = piece[0:whole].reshape(CHUNKS, 16, 128)
            o_ref[:, at * 16 : (at + 1) * 16, :] = main.astype(BF16)
            for group in range(CHUNKS // 8):
                start = whole + group * 16
                tops[group].append(piece[start : start + 16].astype(BF16))
    for group in range(CHUNKS // 8):
        packed = dot(spread, jnp.concatenate(tops[group], axis=0)).reshape(8, 32, 128)
        at = group * 8
        o_ref[at : at + 8, 192:224, :] = packed.astype(BF16)


EXPERT_SCRATCH = [
    pltpu.VMEM((EXPERT_ROWS, D), BF16),
    pltpu.VMEM((EXPERT_ROWS, D), BF16),
]
EXPERT_COST = pl.CostEstimate(
    flops=EXPERT_ROWS * D * D * 4,
    bytes_accessed=2 * CHUNKS * PACK * 128 * 2,
    transcendentals=EXPERT_ROWS * D,
)
HALF = (CHUNKS, PACK, 128)


RESIDENT = pl.BlockSpec(memory_space=pltpu.VMEM)


def fetch_kernel(after_ref, expand_hbm, reduce_hbm, expand, reduce, sems):
    copies = [
        pltpu.make_async_copy(source, target, sems.at[i])
        for i, (source, target) in enumerate(((expand_hbm, expand), (reduce_hbm, reduce)))
    ]
    for copy in copies:
        copy.start()
    for copy in copies:
        copy.wait()


def fetch_weights(after, expand, reduce):
    anywhere = pl.BlockSpec(memory_space=pl.ANY)
    return pl.pallas_call(
        fetch_kernel,
        in_specs=[anywhere] * 3,
        out_specs=[RESIDENT] * 2,
        out_shape=[pltpu.VMEM((1, D, D), BF16)] * 2,
        scratch_shapes=[pltpu.SemaphoreType.DMA((2,))],
        compiler_params=pltpu.CompilerParams(vmem_limit_bytes=1 << 20),
        name="fetch_weights",
    )(after, in_hbm(expand), in_hbm(reduce))


def run_experts(half, arrived, expand, reduce):
    return pl.pallas_call(
        partial(later_kernel, half),
        in_specs=[RESIDENT] * 3,
        out_specs=RESIDENT,
        out_shape=pltpu.VMEM(HALF, BF16),
        scratch_shapes=EXPERT_SCRATCH,
        compiler_params=pltpu.CompilerParams(vmem_limit_bytes=16 << 20),
        cost_estimate=EXPERT_COST,
        name="experts",
    )(in_vmem(arrived), in_vmem(expand), in_vmem(reduce))


def combine_kernel(x_hbm, main_ref, last_ref, gate_ref, space_ref, o_ref, chunks, rows, sems):
    def fetch(part):
        at = pl.ds(part * CHUNKS, CHUNKS)
        return pltpu.make_async_copy(x_hbm.at[at], chunks.at[at], sems.at[part])

    for part in range(2):
        fetch(part).start()
    at = lax.broadcasted_iota(jnp.int32, (2 * ROWS, EXPERT_ROWS), 1)
    in_last = at >= CHUNKS * MAIN
    last_code = ((at - CHUNKS * MAIN) >> 2) * 2 + (at & 1)
    main_code = (at >> 5) * MAIN + (at & 15)
    code = jnp.where(in_last, last_code, main_code)
    wanted = jnp.where(in_last, last_ref[...], main_ref[...])
    step = jnp.where(in_last, CHUNKS, CHUNKS // 2 * MAIN)
    picked = None
    for part in range(2):
        fetch(part).wait()
        half = rows.at[part * EXPERT_ROWS : (part + 1) * EXPERT_ROWS]
        unpack(chunks.at[part * CHUNKS : (part + 1) * CHUNKS], half, CHUNKS)
        chosen = (code + part * step == wanted).astype(F32).astype(BF16)
        term = dot(chosen, half[...])
        picked = term if picked is None else picked + term
    mix = picked[0:ROWS] * gate_ref[:, 0:1] + picked[ROWS:] * gate_ref[:, 1:2]
    o_ref[...] = (space_ref[...] + mix).astype(BF16)


def combine(returned, main, last, gates, after_space):
    return pl.pallas_call(
        combine_kernel,
        in_specs=[pl.BlockSpec(memory_space=pl.ANY)] + [pl.BlockSpec(memory_space=pltpu.VMEM)] * 4,
        out_shape=jax.ShapeDtypeStruct((ROWS, D), BF16),
        scratch_shapes=[
            pltpu.VMEM((2 * CHUNKS, PACK, 128), BF16),
            pltpu.VMEM((2 * EXPERT_ROWS, D), BF16),
            pltpu.SemaphoreType.DMA((2,)),
        ],
        compiler_params=pltpu.CompilerParams(vmem_limit_bytes=VMEM),
        name="combine",
    )(in_hbm(returned), *map(in_vmem, (main, last, gates, after_space)))


def shards(
    patches,
    temporal_q,
    temporal_k,
    temporal_v,
    clip_lengths,
    w_time,
    gain_space,
    w_space,
    w_merge,
    gain_mix,
    expert_ids,
    gate_weights,
    w_expand,
    w_reduce,
):
    frame_axes, chip_axes = ("x", "y"), ("x", "y", "z")
    swap = [(0, 1), (1, 0)]

    own_rows = lax.dynamic_slice(
        w_space,
        (lax.axis_index("z") * 384, lax.axis_index("c") * 144),
        (384, 144),
    ).T
    w_rows = lax.all_gather(own_rows, ("x", "y", "z", "c"), axis=0, tiled=True)
    w_rows = w_rows.reshape(FRAMES, 4, 288, 384)

    qkv_own = jnp.concatenate(
        [a.reshape(FRAMES, 16, D) for a in (temporal_q, temporal_k, temporal_v)], axis=1
    )
    qkv = lax.all_to_all(qkv_own, frame_axes, split_axis=0, concat_axis=0, tiled=True)
    mixed = time_attention(clip_lengths, qkv)
    mixed = lax.all_to_all(mixed, frame_axes, split_axis=0, concat_axis=0, tiled=True)
    after_time, normed = after_time_step(
        mixed.reshape(ROWS, D), patches.reshape(ROWS, D), w_time, gain_space.reshape(1, D)
    )

    expand, reduce = fetch_weights(normed, w_expand, w_reduce)
    normed, expand, reduce = lax.optimization_barrier((normed, expand, reduce))

    experts = expert_ids.reshape(ROWS * 2)
    index = jnp.arange(ROWS * 2, dtype=jnp.int32)
    earlier = (experts[:, None] == experts[None, :]) & (index[None, :] < index[:, None])
    slot = jnp.sum(earlier.astype(jnp.int32), axis=1)
    main = jnp.where(slot < MAIN, experts * MAIN + slot, -1).reshape(ROWS, 2)
    last = jnp.where(slot >= MAIN, experts * 2 + slot - MAIN, -1).reshape(ROWS, 2)

    after_space, outgoing = space_step(
        normed, w_rows, w_merge, after_time, gain_mix.reshape(1, D), main.T, last.T
    )
    arrived = lax.all_to_all(
        outgoing.reshape(64, PACK, 128), chip_axes, split_axis=0, concat_axis=0, tiled=True
    )
    theirs = lax.ppermute(arrived, "c", swap)
    part_own = run_experts(0, arrived, expand, reduce)
    theirs, part_own = lax.optimization_barrier((theirs, part_own))
    part_a = run_experts(0, theirs, expand, reduce)
    back_a = lax.ppermute(part_a, "c", swap)
    part_b = run_experts(1, theirs, expand, reduce)
    back_b = lax.ppermute(part_b, "c", swap)
    part_own_b = run_experts(1, arrived, expand, reduce)
    sums = add_parts(part_own, back_a, part_own_b, back_b)
    returned = lax.all_to_all(sums, chip_axes, split_axis=0, concat_axis=0, tiled=True)
    main, last = (codes.T.reshape(2 * ROWS, 1) for codes in (main, last))
    out = combine(returned, main, last, gate_weights.reshape(ROWS, 2), after_space)
    return out.reshape(patches.shape)


def solution(mesh):
    grid = Mesh(mesh.devices.reshape(4, 4, 4, 2), ("x", "y", "z", "c"))
    frame, clip = ("x", "y"), ("z", "c")
    every = ("x", "y", "z", "c")
    return jax.shard_map(
        shards,
        mesh=grid,
        in_specs=(
            P(frame, clip, None, None),
            P(frame, clip, None, None),
            P(frame, clip, None, None),
            P(frame, clip, None, None),
            P(clip),
            P(),
            P(),
            P(None, frame),
            P(),
            P(),
            P(frame, clip, None, None),
            P(frame, clip, None, None),
            P(every, None, None),
            P(every, None, None),
        ),
        out_specs=P(frame, clip, None, None),
        check_vma=False,
    )
```

```python
import math
from functools import partial

import jax
import jax.numpy as jnp
from jax import lax
from jax.experimental import pallas as pl
from jax.experimental.pallas import tpu as pltpu
from jax.sharding import Mesh, PartitionSpec as P

HEADS = 24
HEAD = 64
EXPERTS = 32
D = 1536
ROWS = 256
FRAMES = 16
MAIN = 16
PACK = 224
BLOCKS = D // 128
EPSILON = 1e-06
F32 = jnp.float32
BF16 = jnp.bfloat16
VMEM = 40 << 20


def dot(a, b):
    return jnp.dot(a, b, preferred_element_type=F32)


def dot_nt(a, b):
    return lax.dot_general(a, b, (((1,), (1,)), ((), ())), preferred_element_type=F32)


def in_vmem(array):
    return pltpu.with_memory_space_constraint(array, pltpu.VMEM)


def in_hbm(array):
    return pltpu.with_memory_space_constraint(array, pltpu.HBM)


def attend_pair(q, k, v, keep=None):
    low = lax.broadcasted_iota(jnp.int32, (ROWS, 128), 1) < HEAD
    zero, one = jnp.zeros((ROWS, 128), BF16), jnp.ones((ROWS, 128), BF16)
    parts = []
    for mine in (low, ~low):
        scores = dot_nt(q, jnp.where(mine, k, zero))
        if keep is not None:
            scores = jnp.where(keep, scores, -1e30)
        top = jnp.max(scores, axis=-1, keepdims=True)
        powers = jnp.exp2((scores - top) * (1.0 / (math.sqrt(HEAD) * math.log(2.0))))
        parts.append(dot(powers.astype(BF16), jnp.where(mine, v, one)))
    sums = pltpu.roll(jnp.where(low, parts[1], parts[0]), HEAD, 1)
    return (jnp.where(low, parts[0], parts[1]) / sums).astype(BF16)


def norm_rows(values, gain):
    centre = values - jnp.mean(values, axis=-1, keepdims=True)
    spread = jnp.mean(centre * centre, axis=-1, keepdims=True)
    return (centre * lax.rsqrt(spread + EPSILON) * gain).astype(BF16)


TIME_PAIRS = 3


def stack_kernel(q_ref, k_ref, v_ref, o_ref, sems):
    copies = [
        pltpu.make_async_copy(ref, o_ref.at[:, pl.ds(i * 16, 16), :], sems.at[i])
        for i, ref in enumerate((q_ref, k_ref, v_ref))
    ]
    for copy in copies:
        copy.start()
    for copy in copies:
        copy.wait()


def stack_rows(q, k, v):
    anywhere = pl.BlockSpec(memory_space=pl.ANY)
    return pl.pallas_call(
        stack_kernel,
        in_specs=[anywhere] * 3,
        out_specs=anywhere,
        out_shape=pltpu.HBM((FRAMES, 48, D), BF16),
        scratch_shapes=[pltpu.SemaphoreType.DMA((3,))],
        compiler_params=pltpu.CompilerParams(vmem_limit_bytes=1 << 20),
        name="stack_rows",
    )(*map(in_hbm, (q, k, v)))


def time_kernel(len_ref, x_ref, o_ref):
    row = lax.broadcasted_iota(jnp.int32, (ROWS, ROWS), 0)
    col = lax.broadcasted_iota(jnp.int32, (ROWS, ROWS), 1)
    keep = ((row & 15) == (col & 15)) & ((col >> 4) < len_ref[0])

    def heads(step, carry):
        for pair in range(TIME_PAIRS):
            lanes = pl.ds(pl.multiple_of((step * TIME_PAIRS + pair) * 128, 128), 128)
            q = x_ref[:, 0:16, lanes].reshape(ROWS, 128)
            k = x_ref[:, 16:32, lanes].reshape(ROWS, 128)
            v = x_ref[:, 32:48, lanes].reshape(ROWS, 128)
            o_ref[:, :, lanes] = attend_pair(q, k, v, keep).reshape(FRAMES, 16, 128)
        return carry

    lax.fori_loop(0, BLOCKS // TIME_PAIRS, heads, 0)


def time_attention(lengths, qkv):
    return pl.pallas_call(
        time_kernel,
        in_specs=[
            pl.BlockSpec(memory_space=pltpu.SMEM),
            pl.BlockSpec(memory_space=pltpu.VMEM),
        ],
        out_shape=jax.ShapeDtypeStruct((FRAMES, 16, D), BF16),
        compiler_params=pltpu.CompilerParams(vmem_limit_bytes=16 << 20),
        name="time_attention",
    )(lengths, in_vmem(qkv))


def after_time_kernel(mixed_ref, patch_ref, w_ref, gain_ref, after_ref, normed_ref):
    after_time = patch_ref[...].astype(F32) + dot(mixed_ref[...], w_ref[...])
    after_ref[...] = after_time
    normed_ref[...] = norm_rows(after_time, gain_ref[...])


def after_time_step(mixed, patches, w_time, gain):
    return pl.pallas_call(
        after_time_kernel,
        out_shape=[
            jax.ShapeDtypeStruct((ROWS, D), F32),
            jax.ShapeDtypeStruct((ROWS, D), BF16),
        ],
        compiler_params=pltpu.CompilerParams(vmem_limit_bytes=24 << 20),
        name="after_time",
    )(mixed, patches, in_hbm(w_time), gain)


def spread_matrix():
    i = lax.broadcasted_iota(jnp.int32, (256, 192), 0)
    j = lax.broadcasted_iota(jnp.int32, (256, 192), 1)
    same = (i >> 5) == ((j & 15) >> 1)
    place = (i & 31) == 2 * (j >> 4) + (j & 1)
    return (same & place).astype(F32).astype(BF16)


def gather_matrix():
    j = lax.broadcasted_iota(jnp.int32, (192, 256), 0)
    i = lax.broadcasted_iota(jnp.int32, (192, 256), 1)
    same = (i >> 5) == ((j & 15) >> 1)
    place = (i & 31) == 2 * (j >> 4) + (j & 1)
    return (same & place).astype(F32).astype(BF16)


def unpack(block_ref, rows_ref, chunks):
    pick = gather_matrix()
    whole = chunks * 16
    for j in range(BLOCKS):
        rows_ref[0:whole, j * 128 : (j + 1) * 128] = block_ref[
            :, j * 16 : (j + 1) * 16, :
        ].reshape(whole, 128)
    for group in range(chunks // 8):
        packed = block_ref[group * 8 : (group + 1) * 8, 192:224, :].reshape(256, 128)
        last = dot(pick, packed).astype(BF16)
        at = whole + group * 16
        for j in range(BLOCKS):
            rows_ref[at : at + 16, j * 128 : (j + 1) * 128] = last[j * 16 : (j + 1) * 16, :]


GROUPS = 4
PAIRS = 4


def space_kernel(
    normed_ref,
    w_hbm,
    merge_hbm,
    after_ref,
    gain_ref,
    main_ref,
    last_ref,
    space_ref,
    send_ref,
    w_rows,
    merge,
    projected,
    spatial,
    total,
    sems,
):
    per_group = FRAMES // GROUPS
    wide = per_group * 288

    def fetch(group, frame, z):
        f = group * per_group + frame
        return pltpu.make_async_copy(
            w_hbm.at[f, z],
            w_rows.at[pl.ds(f * 288, 288), pl.ds(z * 384, 384)],
            sems.at[group],
        )

    pieces = [(frame, z) for frame in range(per_group) for z in range(4)]
    for group in range(GROUPS):
        for frame, z in pieces:
            fetch(group, frame, z).start()
    fetch_merge = pltpu.make_async_copy(merge_hbm, merge, sems.at[GROUPS])
    fetch_merge.start()
    for group in range(GROUPS):
        for frame, z in pieces:
            fetch(group, frame, z).wait()
        rows = slice(group * wide, (group + 1) * wide)
        projected[:, rows] = dot_nt(normed_ref[...], w_rows[rows, :]).astype(BF16)

    def heads(step, carry):
        for pair in range(PAIRS):
            first = pl.multiple_of((step * PAIRS + pair) * 128, 128)
            q, k, v = (
                projected[:, pl.ds(pl.multiple_of(first + part * D, 128), 128)] for part in range(3)
            )
            spatial[:, pl.ds(first, 128)] = attend_pair(q, k, v)
        return carry

    lax.fori_loop(0, BLOCKS // PAIRS, heads, 0)
    fetch_merge.wait()
    after_space = after_ref[...] + dot(spatial[...], merge[...])
    total[...] = after_space
    keep = pltpu.make_async_copy(total, space_ref, sems.at[GROUPS + 1])
    keep.start()
    mixed_in = norm_rows(after_space, gain_ref[...])
    slot = lax.broadcasted_iota(jnp.int32, (512, ROWS), 0)
    chosen = (slot == main_ref[0:1, :]) | (slot == main_ref[1:2, :])
    rows = dot(chosen.astype(F32).astype(BF16), mixed_in).astype(BF16)
    slot = lax.broadcasted_iota(jnp.int32, (64, ROWS), 0)
    chosen = (slot == last_ref[0:1, :]) | (slot == last_ref[1:2, :])
    last = dot(chosen.astype(F32).astype(BF16), mixed_in).astype(BF16)
    for j in range(BLOCKS):
        piece = rows[:, j * 128 : (j + 1) * 128].reshape(EXPERTS, 16, 128)
        for copy in range(2):
            send_ref[:, copy, j * 16 : (j + 1) * 16, :] = piece
    spread = spread_matrix()
    for group in range(4):
        own = last[group * 16 : (group + 1) * 16, :]
        tall = jnp.concatenate([own[:, j * 128 : (j + 1) * 128] for j in range(BLOCKS)], axis=0)
        packed = dot(spread, tall).astype(BF16).reshape(8, 32, 128)
        for copy in range(2):
            send_ref[group * 8 : (group + 1) * 8, copy, 192:224, :] = packed
    keep.wait()


def space_step(normed, w_rows, w_merge, after_time, gain, main, last):
    resident = pl.BlockSpec(memory_space=pltpu.VMEM)
    anywhere = pl.BlockSpec(memory_space=pl.ANY)
    return pl.pallas_call(
        space_kernel,
        in_specs=[resident, anywhere, anywhere] + [resident] * 4,
        out_specs=[anywhere, resident],
        out_shape=[
            pltpu.HBM((ROWS, D), F32),
            pltpu.VMEM((EXPERTS, 2, PACK, 128), BF16),
        ],
        scratch_shapes=[
            pltpu.VMEM((3 * D, D), BF16),
            pltpu.VMEM((D, D), BF16),
            pltpu.VMEM((ROWS, 3 * D), BF16),
            pltpu.VMEM((ROWS, D), BF16),
            pltpu.VMEM((ROWS, D), F32),
            pltpu.SemaphoreType.DMA((GROUPS + 2,)),
        ],
        compiler_params=pltpu.CompilerParams(vmem_limit_bytes=32 << 20),
        name="space_attention",
    )(
        in_vmem(normed),
        in_hbm(w_rows),
        in_hbm(w_merge),
        *(in_vmem(a) for a in (after_time, gain, main, last)),
    )


CHUNKS = 32
EXPERT_ROWS = CHUNKS * 18
CUT = 512
CUTS = D // CUT


def later_kernel(half, x_ref, expand, reduce, o_ref, rows, hidden):
    expert_body(half, x_ref, expand, reduce, o_ref, rows, hidden, lambda n: None)


def add_kernel(own_a, back_a, own_b, back_b, o_ref):
    step = pl.program_id(0)

    @pl.when(step < 2)
    def _():
        o_ref[...] = (own_a[...].astype(F32) + back_a[...].astype(F32)).astype(BF16)

    @pl.when(step >= 2)
    def _():
        o_ref[...] = (own_b[...].astype(F32) + back_b[...].astype(F32)).astype(BF16)


def add_parts(own_a, back_a, own_b, back_b):
    block = (CHUNKS // 2, PACK, 128)
    first = pl.BlockSpec(block, lambda i: (jnp.minimum(i, 1), 0, 0))
    second = pl.BlockSpec(block, lambda i: (jnp.maximum(i - 2, 0), 0, 0))
    return pl.pallas_call(
        add_kernel,
        grid=(4,),
        in_specs=[first, first, second, second],
        out_specs=pl.BlockSpec(block, lambda i: (i, 0, 0)),
        out_shape=pltpu.HBM((2 * CHUNKS, PACK, 128), BF16),
        compiler_params=pltpu.CompilerParams(vmem_limit_bytes=16 << 20),
        name="add_parts",
    )(own_a, back_a, own_b, back_b)


def expert_body(half, x_ref, expand, reduce, o_ref, rows, hidden, ready):
    whole = CHUNKS * 16
    unpack(x_ref.at[half * CHUNKS : (half + 1) * CHUNKS], rows, CHUNKS)
    for n in range(CUTS):
        ready(n)
        inner = dot(rows[...], expand[0, :, n * CUT : (n + 1) * CUT])
        active = inner * (0.5 + 0.5 * lax.erf(inner * math.sqrt(0.5)))
        hidden[:, n * CUT : (n + 1) * CUT] = active.astype(BF16)
    spread = spread_matrix()
    tops = [[] for _ in range(CHUNKS // 8)]
    for n in range(CUTS):
        ready(CUTS + n)
        part = dot(hidden[...], reduce[0, :, n * CUT : (n + 1) * CUT])
        for j in range(CUT // 128):
            at = n * (CUT // 128) + j
            piece = part[:, j * 128 : (j + 1) * 128]
            main = piece[0:whole].reshape(CHUNKS, 16, 128)
            o_ref[:, at * 16 : (at + 1) * 16, :] = main.astype(BF16)
            for group in range(CHUNKS // 8):
                start = whole + group * 16
                tops[group].append(piece[start : start + 16].astype(BF16))
    for group in range(CHUNKS // 8):
        packed = dot(spread, jnp.concatenate(tops[group], axis=0)).reshape(8, 32, 128)
        at = group * 8
        o_ref[at : at + 8, 192:224, :] = packed.astype(BF16)


EXPERT_SCRATCH = [
    pltpu.VMEM((EXPERT_ROWS, D), BF16),
    pltpu.VMEM((EXPERT_ROWS, D), BF16),
]
EXPERT_COST = pl.CostEstimate(
    flops=EXPERT_ROWS * D * D * 4,
    bytes_accessed=2 * CHUNKS * PACK * 128 * 2,
    transcendentals=EXPERT_ROWS * D,
)
HALF = (CHUNKS, PACK, 128)


RESIDENT = pl.BlockSpec(memory_space=pltpu.VMEM)


def fetch_kernel(after_ref, expand_hbm, reduce_hbm, expand, reduce, sems):
    copies = [
        pltpu.make_async_copy(source, target, sems.at[i])
        for i, (source, target) in enumerate(((expand_hbm, expand), (reduce_hbm, reduce)))
    ]
    for copy in copies:
        copy.start()
    for copy in copies:
        copy.wait()


def fetch_weights(after, expand, reduce):
    anywhere = pl.BlockSpec(memory_space=pl.ANY)
    return pl.pallas_call(
        fetch_kernel,
        in_specs=[anywhere] * 3,
        out_specs=[RESIDENT] * 2,
        out_shape=[pltpu.VMEM((1, D, D), BF16)] * 2,
        scratch_shapes=[pltpu.SemaphoreType.DMA((2,))],
        compiler_params=pltpu.CompilerParams(vmem_limit_bytes=1 << 20),
        name="fetch_weights",
    )(after, in_hbm(expand), in_hbm(reduce))


def run_experts(half, arrived, expand, reduce):
    return pl.pallas_call(
        partial(later_kernel, half),
        in_specs=[RESIDENT] * 3,
        out_specs=RESIDENT,
        out_shape=pltpu.VMEM(HALF, BF16),
        scratch_shapes=EXPERT_SCRATCH,
        compiler_params=pltpu.CompilerParams(vmem_limit_bytes=16 << 20),
        cost_estimate=EXPERT_COST,
        name="experts",
    )(in_vmem(arrived), in_vmem(expand), in_vmem(reduce))


def combine_kernel(x_hbm, main_ref, last_ref, gate_ref, space_ref, o_ref, chunks, rows, sems):
    def fetch(part):
        at = pl.ds(part * CHUNKS, CHUNKS)
        return pltpu.make_async_copy(x_hbm.at[at], chunks.at[at], sems.at[part])

    for part in range(2):
        fetch(part).start()
    at = lax.broadcasted_iota(jnp.int32, (2 * ROWS, EXPERT_ROWS), 1)
    in_last = at >= CHUNKS * MAIN
    last_code = ((at - CHUNKS * MAIN) >> 2) * 2 + (at & 1)
    main_code = (at >> 5) * MAIN + (at & 15)
    code = jnp.where(in_last, last_code, main_code)
    wanted = jnp.where(in_last, last_ref[...], main_ref[...])
    step = jnp.where(in_last, CHUNKS, CHUNKS // 2 * MAIN)
    picked = None
    for part in range(2):
        fetch(part).wait()
        half = rows.at[part * EXPERT_ROWS : (part + 1) * EXPERT_ROWS]
        unpack(chunks.at[part * CHUNKS : (part + 1) * CHUNKS], half, CHUNKS)
        chosen = (code + part * step == wanted).astype(F32).astype(BF16)
        term = dot(chosen, half[...])
        picked = term if picked is None else picked + term
    mix = picked[0:ROWS] * gate_ref[:, 0:1] + picked[ROWS:] * gate_ref[:, 1:2]
    o_ref[...] = (space_ref[...] + mix).astype(BF16)


def combine(returned, main, last, gates, after_space):
    return pl.pallas_call(
        combine_kernel,
        in_specs=[pl.BlockSpec(memory_space=pl.ANY)] + [pl.BlockSpec(memory_space=pltpu.VMEM)] * 4,
        out_shape=jax.ShapeDtypeStruct((ROWS, D), BF16),
        scratch_shapes=[
            pltpu.VMEM((2 * CHUNKS, PACK, 128), BF16),
            pltpu.VMEM((2 * EXPERT_ROWS, D), BF16),
            pltpu.SemaphoreType.DMA((2,)),
        ],
        compiler_params=pltpu.CompilerParams(vmem_limit_bytes=VMEM),
        name="combine",
    )(in_hbm(returned), *map(in_vmem, (main, last, gates, after_space)))


def shards(
    patches,
    temporal_q,
    temporal_k,
    temporal_v,
    clip_lengths,
    w_time,
    gain_space,
    w_space,
    w_merge,
    gain_mix,
    expert_ids,
    gate_weights,
    w_expand,
    w_reduce,
):
    frame_axes, chip_axes = ("x", "y"), ("x", "y", "z")
    swap = [(0, 1), (1, 0)]

    own_rows = lax.dynamic_slice(
        w_space,
        (lax.axis_index("z") * 384, lax.axis_index("c") * 144),
        (384, 144),
    ).T
    w_rows = lax.all_gather(own_rows, ("x", "y", "z", "c"), axis=0, tiled=True)
    w_rows = w_rows.reshape(FRAMES, 4, 288, 384)

    qkv_own = stack_rows(*(a.reshape(FRAMES, 16, D) for a in (temporal_q, temporal_k, temporal_v)))
    qkv = lax.all_to_all(qkv_own, frame_axes, split_axis=0, concat_axis=0, tiled=True)
    mixed = time_attention(clip_lengths, qkv)
    mixed = lax.all_to_all(mixed, frame_axes, split_axis=0, concat_axis=0, tiled=True)
    after_time, normed = after_time_step(
        mixed.reshape(ROWS, D), patches.reshape(ROWS, D), w_time, gain_space.reshape(1, D)
    )

    expand, reduce = fetch_weights(normed, w_expand, w_reduce)
    normed, expand, reduce = lax.optimization_barrier((normed, expand, reduce))

    experts = expert_ids.reshape(ROWS * 2)
    index = jnp.arange(ROWS * 2, dtype=jnp.int32)
    earlier = (experts[:, None] == experts[None, :]) & (index[None, :] < index[:, None])
    slot = jnp.sum(earlier.astype(jnp.int32), axis=1)
    main = jnp.where(slot < MAIN, experts * MAIN + slot, -1).reshape(ROWS, 2)
    last = jnp.where(slot >= MAIN, experts * 2 + slot - MAIN, -1).reshape(ROWS, 2)

    after_space, outgoing = space_step(
        normed, w_rows, w_merge, after_time, gain_mix.reshape(1, D), main.T, last.T
    )
    arrived = lax.all_to_all(
        outgoing.reshape(64, PACK, 128), chip_axes, split_axis=0, concat_axis=0, tiled=True
    )
    theirs = lax.ppermute(arrived, "c", swap)
    part_own = run_experts(0, arrived, expand, reduce)
    theirs, part_own = lax.optimization_barrier((theirs, part_own))
    part_a = run_experts(0, theirs, expand, reduce)
    back_a = lax.ppermute(part_a, "c", swap)
    part_b = run_experts(1, theirs, expand, reduce)
    back_b = lax.ppermute(part_b, "c", swap)
    part_own_b = run_experts(1, arrived, expand, reduce)
    sums = add_parts(part_own, back_a, part_own_b, back_b)
    returned = lax.all_to_all(sums, chip_axes, split_axis=0, concat_axis=0, tiled=True)
    main, last = (codes.T.reshape(2 * ROWS, 1) for codes in (main, last))
    out = combine(returned, main, last, gate_weights.reshape(ROWS, 2), after_space)
    return out.reshape(patches.shape)


def solution(mesh):
    grid = Mesh(mesh.devices.reshape(4, 4, 4, 2), ("x", "y", "z", "c"))
    frame, clip = ("x", "y"), ("z", "c")
    every = ("x", "y", "z", "c")
    return jax.shard_map(
        shards,
        mesh=grid,
        in_specs=(
            P(frame, clip, None, None),
            P(frame, clip, None, None),
            P(frame, clip, None, None),
            P(frame, clip, None, None),
            P(clip),
            P(),
            P(),
            P(None, frame),
            P(),
            P(),
            P(frame, clip, None, None),
            P(frame, clip, None, None),
            P(every, None, None),
            P(every, None, None),
        ),
        out_specs=P(frame, clip, None, None),
        check_vma=False,
    )
```
